256 devices in a mesh: slide: 4 (over x_lo, core), rows: 64 (over z, x_hi, y).
Axes of the slice: x: 4 (x_hi: 2, x_lo: 2; x = x_hi * 2 + x_lo), y: 4, z: 8, core: 2. Of those that a mesh axis runs over, the one named last changes fastest.
Arguments:
- features: bfloat16 [4, 192, 2048, 128], P('slide', None, 'rows'), may hold values from -6 to 6
- depth_kernel: float32 [192, 49], replicated, may hold values from -0.875 to 0.875
- depth_bias: float32 [192], replicated, may hold values from -4 to 4
- norm_gain: float32 [192], replicated, may hold values from 0.1 to 1.9
- norm_bias: float32 [192], replicated, may hold values from -3 to 3
- up_weight: bfloat16 [192, 768], replicated, may hold values from -0.4375 to 0.4375
- up_bias: float32 [768], replicated, may hold values from -3 to 3
- down_weight: bfloat16 [768, 192], replicated, may hold values from -0.21875 to 0.21875
- down_bias: float32 [192], replicated, may hold values from -4 to 4
- layer_scale: float32 [192], replicated, may hold values from 0.2 to 1
- tissue: int32 [4, 64, 4], P('slide', 'rows'), may hold values 0 or 1
- aggregator_order: int32 [4, 256], P('slide'), may hold values from 0 to 255, each once within a row
- tile_cotangent: bfloat16 [4, 256, 192], P('slide', 'rows'), may hold values from -6 to 6
Outputs:
- embedding: float32 [4, 256, 192], P('slide', 'rows')
- input_grad: bfloat16 [4, 192, 2048, 128], P('slide', None, 'rows')
- grad_up: float32 [192, 768], replicated
- grad_down: float32 [768, 192], replicated
- grad_kernel: float32 [192, 49], replicated
The draws below stay inside these ranges and needn't reach their ends.
Inputs may be any that keep to these rules, and one draw needn't show every extreme that they name: `aggregator_order`: each slide's row is a permutation of the 256 positions.
All inputs are finite; a program needn't handle non-finite values. No bound on the sum of `tissue` on one device may be relied on, other than what follows from the above.
Results may differ from the reference program's by a relative error of at most 0.0064.
Values may be sent and summed in bfloat16 or wider, within the bound.
No kernel may reach another device: no remote copies, remote signals or barrier semaphores. Data moves between devices by JAX's collectives and lax.ppermute only.
A program may use at most 128 MiB of HBM per device.

```python
import math
import jax
import jax.numpy as jnp
from jax import lax

C = 192
HID = 768
TILE = 32
WIDTH = 128
SLIDES = 4
HEIGHT = 2048
TILES_DEV = 4
TILES = 256


def plant(entries, stream_key, least, top_value):
    place = [jax.random.randint(jax.random.fold_in(stream_key, axis), (), 0, length) for axis, length in enumerate(entries.shape)]
    longest = entries.shape.index(max(entries.shape))
    beside = place[:longest] + [(place[longest] + 1) % entries.shape[longest]] + place[longest + 1:]
    return entries.at[tuple(place)].set(least).at[tuple(beside)].set(top_value)


def steps_of(own_key, shape, split, least, high):
    gain = 1.0
    for dim, parts in split:
        heights = jax.random.uniform(jax.random.fold_in(jax.random.fold_in(own_key, 6), dim), (parts,), jnp.float32, least / len(split), high / len(split))
        gain = gain * jnp.repeat(jnp.exp(heights), shape[dim] // parts).reshape((-1,) + (1,) * (len(shape) - 1 - dim))
    return gain


def normal_values(stream_key, dims, spread, limit, shards=(), held_as=jnp.bfloat16):
    result = spread * jax.random.normal(stream_key, dims, jnp.float32)
    if shards:
        result = result * steps_of(stream_key, dims, shards, -0.22, 0.18)
    return jnp.clip(result, -limit, limit).astype(held_as)


def setup_inputs(seed: int = 0) -> dict:
    key_list = jax.random.split(jax.random.key(seed), 14)
    return {
        "features": normal_values(key_list[0], (SLIDES, C, HEIGHT, WIDTH), 1.0, 6.0, ((0, 4), (2, 64))),
        "depth_kernel": normal_values(key_list[1], (C, 49), 49 ** -0.5, 0.875, (), jnp.float32),
        "depth_bias": normal_values(key_list[2], (C,), 1.0, 4.0, (), jnp.float32),
        "norm_gain": jnp.clip(1.0 + 0.18 * jax.random.normal(key_list[3], (C,), jnp.float32), 0.1, 1.9),
        "norm_bias": normal_values(key_list[4], (C,), 0.5, 3.0, (), jnp.float32),
        "up_weight": normal_values(key_list[5], (C, HID), C ** -0.5, 0.4375),
        "up_bias": normal_values(key_list[6], (HID,), 0.5, 3.0, (), jnp.float32),
        "down_weight": normal_values(key_list[7], (HID, C), HID ** -0.5, 0.21875),
        "down_bias": normal_values(key_list[8], (C,), 1.0, 4.0, (), jnp.float32),
        "layer_scale": jnp.clip(jnp.exp(jax.random.uniform(key_list[9], (C,), jnp.float32, math.log(0.2), math.log(1.0))), 0.2, 1.0),
        "tissue": plant((jax.random.randint(key_list[10], (SLIDES, HEIGHT // TILE, TILES_DEV), 0, 3) < 2).astype(jnp.int32), jax.random.fold_in(key_list[10], 1), 0, 1),
        "aggregator_order": jax.vmap(lambda own: jax.random.permutation(own, TILES))(jax.random.split(key_list[11], SLIDES)).reshape((SLIDES, TILES)).astype(jnp.int32),
        "tile_cotangent": normal_values(key_list[12], (SLIDES, TILES, C), 1.0, 6.0, ((0, 4), (1, 64))),
    }


def depthwise(source, kernel, height, across, mirrored):
    channels = source.shape[0]
    total = jnp.zeros((channels, height, across), jnp.float32)
    for position in range(49):
        row_start = position // 7
        col_start = position % 7
        if mirrored:
            row_start = 6 - row_start
            col_start = 6 - col_start
        window = lax.slice(source, (0, row_start, col_start), (channels, row_start + height, col_start + across))
        total = total + kernel[:, position][:, None, None] * window.astype(jnp.float32)
    return total

def gelu_exact(values):
    return 0.5 * values * (1.0 + jax.scipy.special.erf(values * 0.7071067811865476))

def gelu_slope(values):
    cumulative = 0.5 * (1.0 + jax.scipy.special.erf(values * 0.7071067811865476))
    density = jnp.exp(-0.5 * values * values) * 0.3989422804014327
    return cumulative + values * density

def block_pass(conv_flat, image_flat, pixel_mask, pixel_cotangent, norm_gain, norm_bias, up_weight, up_bias, down_weight, down_bias, layer_scale):
    average = lax.optimization_barrier(jnp.mean(conv_flat, axis=0, keepdims=True))
    centered = conv_flat - average
    variance = lax.optimization_barrier(jnp.mean(centered * centered, axis=0, keepdims=True))
    reciprocal = lax.rsqrt(variance + 1e-06)
    standard = centered * reciprocal
    normed = (standard * norm_gain[:, None] + norm_bias[:, None]).astype(jnp.bfloat16)
    activation_in = jnp.dot(up_weight.T, normed, preferred_element_type=jnp.float32) + up_bias[:, None]
    hidden = gelu_exact(activation_in).astype(jnp.bfloat16)
    branch = jnp.dot(down_weight.T, hidden, preferred_element_type=jnp.float32) + down_bias[:, None]
    scaled_mask = pixel_mask[None, :] * layer_scale[:, None]
    output = image_flat.astype(jnp.float32) + scaled_mask * branch
    grad_branch = (scaled_mask * pixel_cotangent).astype(jnp.bfloat16)
    grad_hidden = jnp.dot(down_weight, grad_branch, preferred_element_type=jnp.float32)
    grad_activation = (grad_hidden * gelu_slope(activation_in)).astype(jnp.bfloat16)
    grad_normed = jnp.dot(up_weight, grad_activation, preferred_element_type=jnp.float32)
    grad_standard = grad_normed * norm_gain[:, None]
    grad_conv = reciprocal * (grad_standard - lax.optimization_barrier(jnp.mean(grad_standard, axis=0, keepdims=True)) - standard * lax.optimization_barrier(jnp.mean(grad_standard * standard, axis=0, keepdims=True)))
    grad_conv = grad_conv.astype(jnp.bfloat16)
    up_term = jnp.dot(normed, grad_activation.T, preferred_element_type=jnp.float32)
    down_term = jnp.dot(grad_branch, hidden.T, preferred_element_type=jnp.float32)
    return (output, grad_conv, up_term, down_term)

def reference(features, depth_kernel, depth_bias, norm_gain, norm_bias, up_weight, up_bias, down_weight, down_bias, layer_scale, tissue, aggregator_order, tile_cotangent):
    loss_norm = 1.0 / math.sqrt(SLIDES * HEIGHT * WIDTH)
    tile_rows = HEIGHT // TILE
    block_pixels = TILE * WIDTH

    def slide_pass(inputs):
        pixels_in, tissue_map, order, cotangent = inputs
        extended = jnp.pad(pixels_in, ((0, 0), (3, 3), (3, 3)))
        convolved = depthwise(extended, depth_kernel, HEIGHT, WIDTH, False) + depth_bias[:, None, None]
        wanted = jnp.take(cotangent, order.astype(jnp.int32), axis=0).astype(jnp.float32)
        wanted = wanted.reshape(tile_rows, TILES_DEV, C)
        masks = tissue_map.astype(jnp.float32)
        conv_rows = convolved.reshape(C, tile_rows, block_pixels).transpose(1, 0, 2)
        image_rows = pixels_in.reshape(C, tile_rows, block_pixels).transpose(1, 0, 2)

        def row_pass(carry, row_inputs):
            conv_flat, image_flat, mask_row, cotangent_row = row_inputs
            pixel_mask = jnp.broadcast_to(mask_row[None, :, None], (TILE, TILES_DEV, TILE)).reshape(block_pixels)
            pixel_cotangent = jnp.broadcast_to(cotangent_row.T[:, None, :, None], (C, TILE, TILES_DEV, TILE)).reshape(C, block_pixels)
            output, grad_conv, up_term, down_term = block_pass(conv_flat, image_flat, pixel_mask, pixel_cotangent, norm_gain, norm_bias, up_weight, up_bias, down_weight, down_bias, layer_scale)
            embedded = lax.optimization_barrier(jnp.mean(output.reshape(C, TILE, TILES_DEV, TILE), axis=(1, 3))).T
            return ((carry[0] + up_term, carry[1] + down_term), (embedded, grad_conv, pixel_cotangent))
        start = (jnp.zeros((C, HID), jnp.float32), jnp.zeros((C, HID), jnp.float32))
        sums, stacked = lax.scan(row_pass, start, (conv_rows, image_rows, masks, wanted))
        embedded, grad_convs, cotangents = stacked
        grad_image = grad_convs.transpose(1, 0, 2).reshape(C, HEIGHT, WIDTH)
        cotangent_image = cotangents.transpose(1, 0, 2).reshape(C, HEIGHT, WIDTH)
        grad_extended = jnp.pad(grad_image, ((0, 0), (3, 3), (3, 3)))
        input_grad = (cotangent_image + depthwise(grad_extended, depth_kernel, HEIGHT, WIDTH, True)).astype(jnp.bfloat16)
        kernel_cols = []
        for position in range(49):
            row_start = position // 7
            col_start = position % 7
            window = lax.slice(extended, (0, row_start, col_start), (C, row_start + HEIGHT, col_start + WIDTH))
            kernel_cols.append(lax.optimization_barrier(jnp.sum(grad_image.astype(jnp.float32) * window.astype(jnp.float32), axis=(1, 2))))
        kernel_term = jnp.stack(kernel_cols, axis=1)
        return (embedded.reshape(TILES, C), input_grad, sums[0], sums[1], kernel_term)
    results = lax.map(slide_pass, (features, tissue, aggregator_order, tile_cotangent))
    grad_up = lax.optimization_barrier(jnp.sum(results[2], axis=0)) * loss_norm
    grad_down = lax.optimization_barrier(jnp.sum(results[3], axis=0)).T * loss_norm
    grad_kernel = lax.optimization_barrier(jnp.sum(results[4], axis=0)) * loss_norm
    return (results[0], results[1], grad_up, grad_down, grad_kernel)
```

```python
import functools
import math

import jax
import jax.numpy as jnp
from jax import lax
from jax.experimental import pallas as pl
from jax.experimental.pallas import tpu as pltpu
from jax.sharding import PartitionSpec as P

TILE = 32
LANES = 128
HIGHEST = lax.Precision.HIGHEST
F32 = jnp.float32
BF16 = jnp.bfloat16


def lane_ids(rows):
    return lax.broadcasted_iota(jnp.int32, (rows, LANES), 1)


def spread_taps(taps, spread_ref, flip):
    lanes = lane_ids(8)
    for a in range(7):
        for b in range(7):
            tap = 7 * (6 - a) + (6 - b) if flip else 7 * a + b
            value = jnp.broadcast_to(taps[:, tap : tap + 1], (8, LANES))
            shift = b - 3
            if shift > 0:
                value = jnp.where(lanes >= shift, value, 0.0)
            elif shift < 0:
                value = jnp.where(lanes < LANES + shift, value, 0.0)
            spread_ref[7 * a + b] = value


def depthwise(source_ref, spread_ref, c0, store, height):
    step = 16
    for first in range(0, height, step):
        rows = [source_ref[first + r, pl.ds(c0, 8), :] for r in range(step + 6)]
        sums = [None] * step
        for b in range(7):
            taps = [spread_ref[7 * a + b] for a in range(7)]
            for i in range(step):
                part = taps[0] * rows[i]
                for a in range(1, 7):
                    part = part + taps[a] * rows[i + a]
                if b != 3:
                    part = pltpu.roll(part, (3 - b) % LANES, 1)
                sums[i] = part if b == 0 else sums[i] + part
        for i in range(step):
            store(first + i, sums[i])


def widen(top_ref, mid_ref, bottom_ref, wide_ref):
    height = mid_ref.shape[0]
    for r in range(3):
        wide_ref[r] = top_ref[r].astype(F32)
        wide_ref[height + 3 + r] = bottom_ref[r].astype(F32)

    def copy(r, carry):
        wide_ref[r + 3] = mid_ref[r].astype(F32)
        return carry

    lax.fori_loop(0, height, copy, 0)


def forward_kernel(
    top_ref, mid_ref, bottom_ref, taps_ref, vectors_ref,
    normed_ref, standard_ref, reciprocal_ref, feature_sum_ref,
    wide_ref, spread_ref,
):
    height, channels, _ = mid_ref.shape
    widen(top_ref, mid_ref, bottom_ref, wide_ref)

    def conv(block, carry):
        c0 = pl.multiple_of(block * 8, 8)
        spread_taps(taps_ref[pl.ds(c0, 8), :], spread_ref, False)
        bias = jnp.broadcast_to(vectors_ref[pl.ds(c0, 8), 0:1], (8, LANES))

        def store(i, value):
            standard_ref[i, pl.ds(c0, 8), :] = value + bias

        depthwise(wide_ref, spread_ref, c0, store, height)
        total = wide_ref[3, pl.ds(c0, 8), :]
        for i in range(1, height):
            total = total + wide_ref[3 + i, pl.ds(c0, 8), :]
        feature_sum_ref[pl.ds(c0, 8), :] = total
        return carry

    lax.fori_loop(0, channels // 8, conv, 0)
    gain = jnp.broadcast_to(vectors_ref[:, 1:2], (channels, LANES))
    shift = jnp.broadcast_to(vectors_ref[:, 2:3], (channels, LANES))
    wide_ref[0] = gain
    wide_ref[1] = shift

    def norm(i, carry):
        values = standard_ref[i]
        average = jnp.sum(values, axis=0, keepdims=True) * (1.0 / channels)
        centered = values - average
        variance = jnp.sum(centered * centered, axis=0, keepdims=True) * (1.0 / channels)
        reciprocal = lax.rsqrt(variance + 1e-06)
        standard = centered * reciprocal
        standard_ref[i] = standard
        reciprocal_ref[pl.ds(i, 1), :] = reciprocal
        normed_ref[i] = (standard * wide_ref[0] + wide_ref[1]).astype(BF16)
        return carry

    lax.fori_loop(0, height, norm, 0)


def gelu_parts(v):
    size = jnp.abs(v)
    t = 1.0 / (1.0 + (0.3275911 * 0.7071067811865476) * size)
    density = jnp.exp(v * v * -0.5)
    poly = t * (
        0.5 * 0.254829592
        + t * (0.5 * -0.284496736 + t * (0.5 * 1.421413741 + t * (0.5 * -1.453152027 + t * (0.5 * 1.061405429))))
    )
    tail = poly * density
    cumulative = jnp.where(v >= 0.0, 1.0 - tail, tail)
    hidden = v * cumulative
    slope = cumulative + v * (density * 0.3989422804014327)
    return hidden, slope


def mlp_kernel(
    normed_ref, standard_ref, reciprocal_ref, feature_sum_ref,
    gathered_ref, meta_ref, vectors_ref, row_vectors_ref,
    up_ref, up_t_ref, down_ref, up_bias_ref,
    grad_conv_ref, part_ref, embedding_ref, cotangent_ref,
    pre_ref, grad_ref, slope_scale_ref, bias_ref, hidden_sum_ref, up_sum_ref, gain_ref,
    *, scale,
):
    height, channels, _ = normed_ref.shape
    hidden_units = down_ref.shape[0]
    tiles = gathered_ref.shape[0]
    picks = lax.broadcasted_iota(jnp.int32, (8, tiles), 1) == meta_ref[:, 0:1]
    wanted = jnp.dot(picks.astype(BF16), gathered_ref[...], preferred_element_type=F32)
    mask = meta_ref[:, 1:2].astype(F32)
    scaled_mask = mask * row_vectors_ref[0:1, :]
    branch_rows = (scaled_mask * wanted).astype(BF16)
    member = lax.broadcasted_iota(jnp.int32, (8, LANES), 1) // TILE == lax.broadcasted_iota(
        jnp.int32, (8, LANES), 0
    )
    member_f32 = member.astype(F32)
    first = (((0,), (0,)), ((), ()))
    last = (((1,), (1,)), ((), ()))
    grad_branch = lax.dot_general(
        branch_rows.astype(F32), member_f32, first, precision=HIGHEST, preferred_element_type=F32
    ).astype(BF16)
    cotangent_ref[...] = lax.dot_general(
        wanted, member_f32, first, precision=HIGHEST, preferred_element_type=F32
    )
    slope_scale_ref[...] = jnp.dot(down_ref[...], grad_branch, preferred_element_type=F32)
    bias_ref[...] = jnp.broadcast_to(up_bias_ref[...], (hidden_units, LANES))
    gain_ref[...] = jnp.broadcast_to(vectors_ref[:, 1:2], (channels, LANES))
    hidden_sum_ref[...] = jnp.zeros_like(hidden_sum_ref)
    up_sum_ref[...] = jnp.zeros_like(up_sum_ref)
    chunk = 256
    step = 2

    def rows(block, carry):
        r0 = block * step
        normed = jnp.concatenate([normed_ref[r0 + r] for r in range(step)], axis=1)
        grad_normed = None
        for f0 in range(0, hidden_units, chunk):
            pre_ref[f0 : f0 + chunk, :] = jnp.dot(
                up_t_ref[f0 : f0 + chunk, :], normed, preferred_element_type=F32
            )
        for f0 in range(0, hidden_units, chunk):
            for f in range(f0, f0 + chunk, 16):
                total = hidden_sum_ref[f : f + 16, :]
                for r in range(step):
                    cols = slice(r * LANES, (r + 1) * LANES)
                    hidden, slope = gelu_parts(pre_ref[f : f + 16, cols] + bias_ref[f : f + 16, :])
                    total = total + hidden
                    grad_ref[f : f + 16, cols] = (slope_scale_ref[f : f + 16, :] * slope).astype(BF16)
                hidden_sum_ref[f : f + 16, :] = total
            grad = grad_ref[f0 : f0 + chunk, :]
            term = jnp.dot(up_ref[:, f0 : f0 + chunk], grad, preferred_element_type=F32)
            grad_normed = term if grad_normed is None else grad_normed + term
            up_sum_ref[:, f0 : f0 + chunk] += lax.dot_general(
                normed, grad, last, preferred_element_type=F32
            )
        for r in range(step):
            grad_standard = grad_normed[:, r * LANES : (r + 1) * LANES] * gain_ref[...]
            standard = standard_ref[r0 + r]
            m1 = jnp.sum(grad_standard, axis=0, keepdims=True) * (1.0 / channels)
            m2 = jnp.sum(grad_standard * standard, axis=0, keepdims=True) * (1.0 / channels)
            grad_conv_ref[r0 + r] = (
                reciprocal_ref[pl.ds(r0 + r, 1), :] * (grad_standard - m1 - standard * m2)
            ).astype(BF16)
        return carry

    lax.fori_loop(0, height // step, rows, 0)
    hidden_rows = lax.dot_general(
        member_f32, hidden_sum_ref[...], last, precision=HIGHEST, preferred_element_type=F32
    )
    inverse = 1.0 / (height * TILE)
    branch = jnp.dot(
        hidden_rows * inverse, down_ref[...].astype(F32), precision=HIGHEST, preferred_element_type=F32
    ) + row_vectors_ref[1:2, :]
    features = lax.dot_general(
        member_f32, feature_sum_ref[...], last, precision=HIGHEST, preferred_element_type=F32
    )
    embedding_ref[...] = features * inverse + scaled_mask * branch
    down_sum = lax.dot_general(
        branch_rows.astype(F32), hidden_rows * scale, first, precision=HIGHEST, preferred_element_type=F32
    )
    across = hidden_units // LANES
    half = (channels // 8) * across
    for r in range(channels // 8):
        for k in range(across):
            at = (r * across + k) * 8
            cols = slice(k * LANES, (k + 1) * LANES)
            part_ref[at : at + 8, :] = up_sum_ref[8 * r : 8 * r + 8, cols] * scale
            part_ref[half * 8 + at : half * 8 + at + 8, :] = down_sum[8 * r : 8 * r + 8, cols]


def kernel_grad_kernel(
    top_ref, mid_ref, bottom_ref, grad_ref, out_ref, wide_ref, wide_grad_ref, *, scale
):
    height, channels, _ = mid_ref.shape
    widen(top_ref, mid_ref, bottom_ref, wide_ref)

    def copy(r, carry):
        wide_grad_ref[r] = grad_ref[r].astype(F32)
        return carry

    lax.fori_loop(0, height, copy, 0)
    lanes = lane_ids(8)

    def conv(block, carry):
        c0 = pl.multiple_of(block * 8, 8)
        out = jnp.zeros((8, LANES), F32)
        for b in range(7):
            shift = b - 3
            sums = [None] * 7
            for i in range(height):
                grad = wide_grad_ref[i, pl.ds(c0, 8), :]
                if shift != 0:
                    grad = pltpu.roll(grad, shift % LANES, 1)
                for a in range(7):
                    term = grad * wide_ref[i + a, pl.ds(c0, 8), :]
                    sums[a] = term if i == 0 else sums[a] + term
            for a in range(7):
                total = sums[a]
                if shift > 0:
                    total = jnp.where(lanes >= shift, total, 0.0)
                elif shift < 0:
                    total = jnp.where(lanes < LANES + shift, total, 0.0)
                total = jnp.sum(total, axis=1, keepdims=True)
                out = jnp.where(lanes == 7 * a + b, total, out)
        out_ref[pl.ds(c0, 8), :] = out * scale
        return carry

    lax.fori_loop(0, channels // 8, conv, 0)


def input_grad_kernel(
    top_ref, mid_ref, bottom_ref, taps_ref, cotangent_ref, out_ref, wide_ref, spread_ref, sum_ref
):
    height, channels, _ = mid_ref.shape
    widen(top_ref, mid_ref, bottom_ref, wide_ref)

    def conv(block, carry):
        c0 = pl.multiple_of(block * 8, 8)
        spread_taps(taps_ref[pl.ds(c0, 8), :], spread_ref, True)
        cotangent = cotangent_ref[pl.ds(c0, 8), :]

        def store(i, value):
            sum_ref[i, pl.ds(c0, 8), :] = value + cotangent

        depthwise(wide_ref, spread_ref, c0, store, height)
        return carry

    lax.fori_loop(0, channels // 8, conv, 0)

    def copy(r, carry):
        out_ref[r] = sum_ref[r].astype(BF16)
        return carry

    lax.fori_loop(0, height, copy, 0)


PARAMS = pltpu.CompilerParams(vmem_limit_bytes=48 * 1024 * 1024)


def cost(us):
    return pl.CostEstimate(flops=int(us * 1.0e9), bytes_accessed=4 << 20, transcendentals=0)


def whole(x):
    return pl.BlockSpec(x.shape, lambda i, n=x.ndim: (0,) * n)


def piece(shape, dim, k):
    return pl.BlockSpec(shape, lambda i, n=len(shape): tuple(k if d == dim else 0 for d in range(n)))


def shapes_of(*pairs):
    return [jax.ShapeDtypeStruct(s, d) for s, d in pairs]


def exchange(x, axis, pattern):
    n = lax.axis_size(axis)
    return lax.ppermute(x, axis, [(i, i ^ pattern) for i in range(n)])


def rank_in(bits, index):
    rank = 0
    for k, bit in enumerate(bits):
        rank = rank + ((index // bit) % 2) * (1 << k)
    return rank


def patterns(bits):
    return [sum(bit for k, bit in enumerate(bits) if (p >> k) & 1) for p in range(1 << len(bits))]


def tree(parts):
    while len(parts) > 1:
        parts = [parts[k] + parts[k + 1] for k in range(0, len(parts), 2)]
    return parts[0]


def scatter_sum(x, axis, bits):
    ways = 1 << len(bits)
    size = x.shape[0] // ways
    me = rank_in(bits, lax.axis_index(axis))
    parts = []
    for k, pattern in enumerate(patterns(bits)):
        part = lax.dynamic_slice_in_dim(x, (me ^ k) * size, size)
        parts.append(part if k == 0 else exchange(part, axis, pattern))
    return tree(parts)


def full_sum(x, axis, bits):
    return tree([x if k == 0 else exchange(x, axis, p) for k, p in enumerate(patterns(bits))])


def gather(x, axis, bits):
    ways = 1 << len(bits)
    size = x.shape[0]
    me = rank_in(bits, lax.axis_index(axis))
    out = jnp.zeros((size * ways,) + x.shape[1:], x.dtype)
    for k, pattern in enumerate(patterns(bits)):
        part = x if k == 0 else exchange(x, axis, pattern)
        out = lax.dynamic_update_slice_in_dim(out, part, (me ^ k) * size, 0)
    return out


SCATTER = (("slide", (1,)), ("rows", (1, 2)), ("rows", (8, 16)))
REST = (("rows", (4, 32)), ("slide", (2,)))


def sum_all(x):
    for axis, bits in SCATTER:
        x = scatter_sum(x, axis, bits)
    for axis, bits in REST:
        x = full_sum(x, axis, bits)
    for axis, bits in reversed(SCATTER):
        x = gather(x, axis, bits)
    return x


def sum_small(x):
    for axis, bits in (("slide", (1, 2)), ("rows", (1, 2)), ("rows", (4, 8)), ("rows", (16, 32))):
        x = full_sum(x, axis, bits)
    return x


def edges(rows):
    count = lax.axis_size("rows")
    top = lax.ppermute(rows[-3:], "rows", [(i, i + 1) for i in range(count - 1)])
    bottom = lax.ppermute(rows[:3], "rows", [(i + 1, i) for i in range(count - 1)])
    return top, bottom


def on_device(
    features,
    depth_kernel,
    depth_bias,
    norm_gain,
    norm_bias,
    up_weight,
    up_bias,
    down_weight,
    down_bias,
    layer_scale,
    tissue,
    aggregator_order,
    tile_cotangent,
):
    channels, height, across = features.shape[1:]
    hidden_units = up_weight.shape[1]
    row_count = lax.axis_size("rows")
    tiles_here = across // TILE
    scale = 1.0 / math.sqrt(lax.axis_size("slide") * row_count * height * across)

    image = features[0].transpose(1, 0, 2)
    top, bottom = edges(image)
    sent = jnp.broadcast_to(tile_cotangent, (row_count,) + tile_cotangent.shape[1:])
    gathered = lax.all_to_all(sent, "rows", 0, 0, tiled=True).reshape(-1, channels)
    positions = lax.dynamic_slice_in_dim(
        aggregator_order[0], lax.axis_index("rows") * tiles_here, tiles_here
    )
    meta = jnp.pad(jnp.stack([positions, tissue[0, 0]], axis=1), ((0, 8 - tiles_here), (0, 0)))
    vectors = jnp.stack([depth_bias, norm_gain, norm_bias], axis=1)
    row_vectors = jnp.stack([layer_scale, down_bias], axis=0)
    up_t = up_weight.T

    image_shape = (height, channels, across)
    wide = pltpu.VMEM((height + 6, channels, across), F32)
    spread = pltpu.VMEM((49, 8, LANES), F32)
    operands = (top, image, bottom, depth_kernel, vectors)
    normed, standard, reciprocal, feature_sum = pl.pallas_call(
        forward_kernel,
        grid=(1,),
        in_specs=[whole(x) for x in operands],
        out_specs=[
            pl.BlockSpec(image_shape, lambda i: (0, 0, 0)),
            pl.BlockSpec(image_shape, lambda i: (0, 0, 0)),
            pl.BlockSpec((height, across), lambda i: (0, 0)),
            pl.BlockSpec((channels, across), lambda i: (0, 0)),
        ],
        out_shape=shapes_of(
            (image_shape, BF16), (image_shape, F32), ((height, across), F32), ((channels, across), F32)
        ),
        scratch_shapes=[wide, spread],
        compiler_params=PARAMS,
        cost_estimate=cost(20),
        name="conv_norm",
    )(*operands)

    operands = (
        normed, standard, reciprocal, feature_sum, gathered, meta, vectors, row_vectors,
        up_weight, up_t, down_weight, up_bias[:, None],
    )
    part_rows = 2 * channels * hidden_units // LANES
    grad_conv, part, embedding, cotangent = pl.pallas_call(
        functools.partial(mlp_kernel, scale=scale),
        grid=(1,),
        in_specs=[whole(x) for x in operands],
        out_specs=[
            pl.BlockSpec(image_shape, lambda i: (0, 0, 0)),
            pl.BlockSpec((part_rows, LANES), lambda i: (0, 0)),
            pl.BlockSpec((8, channels), lambda i: (0, 0)),
            pl.BlockSpec((channels, across), lambda i: (0, 0)),
        ],
        out_shape=shapes_of(
            (image_shape, BF16), ((part_rows, LANES), F32), ((8, channels), F32), ((channels, across), F32)
        ),
        scratch_shapes=[
            pltpu.VMEM((hidden_units, 2 * LANES), F32),
            pltpu.VMEM((hidden_units, 2 * LANES), BF16),
            pltpu.VMEM((hidden_units, LANES), F32),
            pltpu.VMEM((hidden_units, LANES), F32),
            pltpu.VMEM((hidden_units, LANES), F32),
            pltpu.VMEM((channels, hidden_units), F32),
            pltpu.VMEM((channels, LANES), F32),
        ],
        compiler_params=PARAMS,
        cost_estimate=cost(30),
        name="mlp_both_ways",
    )(*operands)

    grad_top, grad_bottom = edges(grad_conv)
    pieces = 2
    size = channels // pieces
    kernel_terms = []
    grads = []
    for k in range(pieces):
        kernel_terms.append(
            pl.pallas_call(
                functools.partial(kernel_grad_kernel, scale=scale),
                grid=(1,),
                in_specs=[
                    piece((3, size, across), 1, k),
                    piece((height, size, across), 1, k),
                    piece((3, size, across), 1, k),
                    piece((height, size, across), 1, k),
                ],
                out_specs=pl.BlockSpec((size, LANES), lambda i: (0, 0)),
                out_shape=jax.ShapeDtypeStruct((size, LANES), F32),
                scratch_shapes=[
                    pltpu.VMEM((height + 6, size, across), F32),
                    pltpu.VMEM((height, size, across), F32),
                ],
                compiler_params=PARAMS,
                cost_estimate=cost(8),
                name="kernel_grad",
            )(top, image, bottom, grad_conv)
        )
    for k in range(pieces):
        grads.append(
            pl.pallas_call(
                input_grad_kernel,
                grid=(1,),
                in_specs=[
                    piece((3, size, across), 1, k),
                    piece((height, size, across), 1, k),
                    piece((3, size, across), 1, k),
                    piece((size, 49), 0, k),
                    piece((size, across), 0, k),
                ],
                out_specs=pl.BlockSpec((height, size, across), lambda i: (0, 0, 0)),
                out_shape=jax.ShapeDtypeStruct((height, size, across), BF16),
                scratch_shapes=[
                    pltpu.VMEM((height + 6, size, across), F32),
                    spread,
                    pltpu.VMEM((height, size, across), F32),
                ],
                compiler_params=PARAMS,
                cost_estimate=cost(8),
                name="input_grad",
            )(grad_top, grad_conv, grad_bottom, depth_kernel, cotangent)
        )
    input_grad = jnp.concatenate(grads, axis=1).transpose(1, 0, 2)[None]

    totals = sum_all(part)
    small = sum_small(jnp.concatenate(kernel_terms, axis=0))
    tiled = totals.reshape(2, channels // 8, hidden_units // LANES, 8, LANES)
    tiled = tiled.transpose(0, 1, 3, 2, 4).reshape(2, channels, hidden_units)
    return (embedding[None, :tiles_here], input_grad, tiled[0], tiled[1].T, small[:, :49])


def solution(mesh):
    return jax.shard_map(
        on_device,
        mesh=mesh,
        in_specs=(
            P("slide", None, "rows", None),
            P(),
            P(),
            P(),
            P(),
            P(),
            P(),
            P(),
            P(),
            P(),
            P("slide", "rows", None),
            P("slide", None),
            P("slide", "rows", None),
        ),
        out_specs=(P("slide", "rows", None), P("slide", None, "rows", None), P(), P(), P()),
        check_vma=False,
    )
```

```python
import functools
import math

import jax
import jax.numpy as jnp
from jax import lax
from jax.experimental import pallas as pl
from jax.experimental.pallas import tpu as pltpu
from jax.sharding import PartitionSpec as P

TILE = 32
LANES = 128
HIGHEST = lax.Precision.HIGHEST
F32 = jnp.float32
BF16 = jnp.bfloat16


def lane_ids(rows):
    return lax.broadcasted_iota(jnp.int32, (rows, LANES), 1)


def spread_taps(taps, spread_ref, flip):
    lanes = lane_ids(8)
    for a in range(7):
        for b in range(7):
            tap = 7 * (6 - a) + (6 - b) if flip else 7 * a + b
            value = jnp.broadcast_to(taps[:, tap : tap + 1], (8, LANES))
            shift = b - 3
            if shift > 0:
                value = jnp.where(lanes >= shift, value, 0.0)
            elif shift < 0:
                value = jnp.where(lanes < LANES + shift, value, 0.0)
            spread_ref[7 * a + b] = value


def depthwise(source_ref, spread_ref, c0, store, height):
    step = 16
    for first in range(0, height, step):
        rows = [source_ref[first + r, pl.ds(c0, 8), :] for r in range(step + 6)]
        sums = [None] * step
        for b in range(7):
            taps = [spread_ref[7 * a + b] for a in range(7)]
            for i in range(step):
                part = taps[0] * rows[i]
                for a in range(1, 7):
                    part = part + taps[a] * rows[i + a]
                if b != 3:
                    part = pltpu.roll(part, (3 - b) % LANES, 1)
                sums[i] = part if b == 0 else sums[i] + part
        for i in range(step):
            store(first + i, sums[i])


def widen(top_ref, mid_ref, bottom_ref, wide_ref):
    height = mid_ref.shape[0]
    for r in range(3):
        wide_ref[r] = top_ref[r].astype(F32)
        wide_ref[height + 3 + r] = bottom_ref[r].astype(F32)

    def copy(r, carry):
        wide_ref[r + 3] = mid_ref[r].astype(F32)
        return carry

    lax.fori_loop(0, height, copy, 0)


def forward_kernel(
    top_ref, mid_ref, bottom_ref, taps_ref, vectors_ref, out_ref, feature_sum_ref, wide_ref, spread_ref
):
    height, channels, _ = mid_ref.shape
    widen(top_ref, mid_ref, bottom_ref, wide_ref)

    def conv(block, carry):
        c0 = pl.multiple_of(block * 8, 8)
        spread_taps(taps_ref[pl.ds(c0, 8), :], spread_ref, False)
        bias = jnp.broadcast_to(vectors_ref[pl.ds(c0, 8), 0:1], (8, LANES))

        def store(i, value):
            out_ref[i, pl.ds(c0, 8), :] = value + bias

        depthwise(wide_ref, spread_ref, c0, store, height)
        total = wide_ref[3, pl.ds(c0, 8), :]
        for i in range(1, height):
            total = total + wide_ref[3 + i, pl.ds(c0, 8), :]
        feature_sum_ref[pl.ds(c0, 8), :] = total
        return carry

    lax.fori_loop(0, channels // 8, conv, 0)


def gelu_parts(v):
    cumulative = 0.5 + 0.5 * lax.erf(v * 0.7071067811865476)
    density = jnp.exp(v * v * -0.5)
    return v * cumulative, cumulative + v * (density * 0.3989422804014327)


def mlp_kernel(
    conv_ref, feature_sum_ref, gathered_ref, meta_ref, vectors_ref, row_vectors_ref,
    up_ref, up_t_ref, down_ref, up_bias_ref,
    grad_conv_ref, part_ref, embedding_ref, cotangent_ref,
    pre_ref, grad_ref, slope_scale_ref, bias_ref, hidden_sum_ref, up_sum_ref, gain_ref,
    normed_ref, standard_ref, reciprocal_ref,
    *, scale,
):
    height = conv_ref.shape[0]
    channels = vectors_ref.shape[0]
    hidden_units = down_ref.shape[0]
    tiles = gathered_ref.shape[0]
    picks = lax.broadcasted_iota(jnp.int32, (8, tiles), 1) == meta_ref[:, 0:1]
    wanted = jnp.dot(picks.astype(BF16), gathered_ref[...], preferred_element_type=F32)
    mask = meta_ref[:, 1:2].astype(F32)
    scaled_mask = mask * row_vectors_ref[0:1, :]
    branch_rows = (scaled_mask * wanted).astype(BF16)
    member = lax.broadcasted_iota(jnp.int32, (8, LANES), 1) // TILE == lax.broadcasted_iota(
        jnp.int32, (8, LANES), 0
    )
    member_f32 = member.astype(F32)
    first = (((0,), (0,)), ((), ()))
    last = (((1,), (1,)), ((), ()))
    grad_branch = lax.dot_general(
        branch_rows.astype(F32), member_f32, first, precision=HIGHEST, preferred_element_type=F32
    ).astype(BF16)
    cotangent_ref[...] = lax.dot_general(
        wanted, member_f32, first, precision=HIGHEST, preferred_element_type=F32
    )
    slope_scale_ref[...] = jnp.dot(down_ref[...], grad_branch, preferred_element_type=F32)
    bias_ref[...] = jnp.broadcast_to(up_bias_ref[...], (hidden_units, LANES))
    gain_ref[0] = jnp.broadcast_to(vectors_ref[:, 1:2], (channels, LANES))
    gain_ref[1] = jnp.broadcast_to(vectors_ref[:, 2:3], (channels, LANES))
    hidden_sum_ref[...] = jnp.zeros_like(hidden_sum_ref)
    up_sum_ref[...] = jnp.zeros_like(up_sum_ref)
    chunk = 256
    step = 2

    blocks = height // step

    def norm(block, slot):
        for r in range(step):
            row = block * step + r
            values = conv_ref[row]
            average = jnp.sum(values, axis=0, keepdims=True) * (1.0 / channels)
            centered = values - average
            variance = jnp.sum(centered * centered, axis=0, keepdims=True) * (1.0 / channels)
            reciprocal = lax.rsqrt(variance + 1e-06)
            standard = centered * reciprocal
            standard_ref[slot, r] = standard
            reciprocal_ref[slot, r : r + 1, :] = reciprocal
            normed_ref[slot, :, r * LANES : (r + 1) * LANES] = (standard * gain_ref[0] + gain_ref[1]).astype(BF16)

    def enter(slot, f0, normed):
        pre_ref[slot, f0 : f0 + chunk, :] = jnp.dot(
            up_t_ref[f0 : f0 + chunk, :], normed, preferred_element_type=F32
        )

    def leave(block, slot, following):
        r0 = block * step
        normed = normed_ref[slot]
        norm(following, 1 - slot)
        after = normed_ref[1 - slot]
        grad_normed = None
        for f0 in range(0, hidden_units, chunk):
            enter(1 - slot, f0, after)
            for f in range(f0, f0 + chunk, 16):
                total = hidden_sum_ref[f : f + 16, :]
                for r in range(step):
                    cols = slice(r * LANES, (r + 1) * LANES)
                    hidden, slope = gelu_parts(pre_ref[slot, f : f + 16, cols] + bias_ref[f : f + 16, :])
                    total = total + hidden
                    grad_ref[slot, f : f + 16, cols] = (slope_scale_ref[f : f + 16, :] * slope).astype(BF16)
                hidden_sum_ref[f : f + 16, :] = total
            grad = grad_ref[slot, f0 : f0 + chunk, :]
            term = jnp.dot(up_ref[:, f0 : f0 + chunk], grad, preferred_element_type=F32)
            grad_normed = term if grad_normed is None else grad_normed + term
            up_sum_ref[:, f0 : f0 + chunk] += lax.dot_general(
                normed, grad, last, preferred_element_type=F32
            )
        for r in range(step):
            grad_standard = grad_normed[:, r * LANES : (r + 1) * LANES] * gain_ref[0]
            standard = standard_ref[slot, r]
            m1 = jnp.sum(grad_standard, axis=0, keepdims=True) * (1.0 / channels)
            m2 = jnp.sum(grad_standard * standard, axis=0, keepdims=True) * (1.0 / channels)
            grad_conv_ref[r0 + r] = (
                reciprocal_ref[slot, r : r + 1, :] * (grad_standard - m1 - standard * m2)
            ).astype(BF16)

    norm(0, 0)
    start = normed_ref[0]
    for f0 in range(0, hidden_units, chunk):
        enter(0, f0, start)

    def pair(k, carry):
        leave(2 * k, 0, 2 * k + 1)
        leave(2 * k + 1, 1, jnp.minimum(2 * k + 2, blocks - 1))
        return carry

    lax.fori_loop(0, blocks // 2, pair, 0)
    hidden_rows = lax.dot_general(
        member_f32, hidden_sum_ref[...], last, precision=HIGHEST, preferred_element_type=F32
    )
    inverse = 1.0 / (height * TILE)
    branch = jnp.dot(
        hidden_rows * inverse, down_ref[...].astype(F32), precision=HIGHEST, preferred_element_type=F32
    ) + row_vectors_ref[1:2, :]
    features = lax.dot_general(
        member_f32, feature_sum_ref[...], last, precision=HIGHEST, preferred_element_type=F32
    )
    embedding_ref[...] = features * inverse + scaled_mask * branch
    down_sum = lax.dot_general(
        branch_rows.astype(F32), hidden_rows * scale, first, precision=HIGHEST, preferred_element_type=F32
    )
    across = hidden_units // LANES
    half = (channels // 8) * across
    for r in range(channels // 8):
        for k in range(across):
            at = (r * across + k) * 8
            cols = slice(k * LANES, (k + 1) * LANES)
            part_ref[at : at + 8, :] = up_sum_ref[8 * r : 8 * r + 8, cols] * scale
            part_ref[half * 8 + at : half * 8 + at + 8, :] = down_sum[8 * r : 8 * r + 8, cols]


def kernel_grad_kernel(
    top_ref, mid_ref, bottom_ref, grad_ref, out_ref, wide_ref, wide_grad_ref, tiles_ref, *, scale, lane0
):
    height, channels, _ = mid_ref.shape
    widen(top_ref, mid_ref, bottom_ref, wide_ref)

    def copy(r, carry):
        wide_grad_ref[r] = grad_ref[r].astype(F32)
        return carry

    lax.fori_loop(0, height, copy, 0)
    lanes = lane_ids(8)

    def conv(block, carry):
        c0 = pl.multiple_of(block * 8, 8)
        for b in range(7):
            shift = b - 3
            sums = [None] * 7
            for i in range(height):
                grad = wide_grad_ref[i, pl.ds(c0, 8), :]
                if shift != 0:
                    grad = pltpu.roll(grad, shift % LANES, 1)
                for a in range(7):
                    term = grad * wide_ref[i + a, pl.ds(c0, 8), :]
                    sums[a] = term if i == 0 else sums[a] + term
            for a in range(7):
                tiles_ref[7 * a + b] = sums[a]
        out = jnp.zeros((8, LANES), F32)
        for tap in range(49):
            shift = tap % 7 - 3
            total = tiles_ref[tap]
            if shift > 0:
                total = jnp.where(lanes >= shift, total, 0.0)
            elif shift < 0:
                total = jnp.where(lanes < LANES + shift, total, 0.0)
            total = jnp.sum(total, axis=1, keepdims=True)
            out = jnp.where(lanes == lane0 + tap, total, out)
        out_ref[pl.ds(c0, 8), :] = out * scale
        return carry

    lax.fori_loop(0, channels // 8, conv, 0)


def input_grad_kernel(
    top_ref, mid_ref, bottom_ref, taps_ref, cotangent_ref, out_ref, wide_ref, spread_ref, sum_ref
):
    height, channels, _ = mid_ref.shape
    widen(top_ref, mid_ref, bottom_ref, wide_ref)

    def conv(block, carry):
        c0 = pl.multiple_of(block * 8, 8)
        spread_taps(taps_ref[pl.ds(c0, 8), :], spread_ref, True)
        cotangent = cotangent_ref[pl.ds(c0, 8), :]

        def store(i, value):
            sum_ref[pl.ds(i, 8, stride=height), :] = value + cotangent

        depthwise(wide_ref, spread_ref, c0, store, height)
        at = pl.multiple_of(c0 * height, 8 * height)
        out_ref[pl.ds(at, 8 * height), :] = sum_ref[...].astype(BF16)
        return carry

    lax.fori_loop(0, channels // 8, conv, 0)


CONV_COST = 0.01
CONV_MIB = 58


def cost(us):
    return pl.CostEstimate(flops=int(us * 1.0e9), bytes_accessed=1 << 20, transcendentals=0)


def whole(x):
    return (x, x.shape, None, 0)


def part_of(x, dim, size, k):
    return (x, tuple(size if d == dim else n for d, n in enumerate(x.shape)), dim, k)


def call(kernel, operands, shapes, scratch, us, name, mib=40):
    def spec(shape, dim=None, k=0):
        return pl.BlockSpec(shape, lambda i: tuple(k if d == dim else 0 for d in range(len(shape))))

    return pl.pallas_call(
        kernel,
        grid=(1,),
        in_specs=[spec(*operand[1:]) for operand in operands],
        out_specs=[spec(shape) for shape, _ in shapes],
        out_shape=[jax.ShapeDtypeStruct(*shape) for shape in shapes],
        scratch_shapes=scratch,
        compiler_params=pltpu.CompilerParams(vmem_limit_bytes=mib << 20),
        cost_estimate=cost(us),
        name=name,
    )(*[operand[0] for operand in operands])


def after(xs, *others):
    return lax.optimization_barrier((tuple(xs), others))[0]


def patterns(bits):
    return [sum(bit for k, bit in enumerate(bits) if (p >> k) & 1) for p in range(1, 1 << len(bits))]


def exchange(x, axis, pattern):
    return lax.ppermute(x, axis, [(i, i ^ pattern) for i in range(lax.axis_size(axis))])


def rank_in(axis, bits):
    index = lax.axis_index(axis)
    return sum(((index // bit) % 2) * (1 << k) for k, bit in enumerate(bits))


def run(x, k, count):
    size = x.shape[0] // count
    return lax.dynamic_slice_in_dim(x, k * size, size)


def tree(parts):
    while len(parts) > 1:
        parts = [parts[k] + parts[k + 1] for k in range(0, len(parts), 2)]
    return parts[0]


def send_parts(x, axis, bits):
    me = rank_in(axis, bits)
    count = 1 << len(bits)
    sent = [exchange(run(x, me ^ (k + 1), count), axis, p) for k, p in enumerate(patterns(bits))]
    return [run(x, me, count)] + sent


def send_all(x, axis, bits):
    return [x] + [exchange(x, axis, p) for p in patterns(bits)]


def in_order(parts, axis, bits):
    me = rank_in(axis, bits)
    size = parts[0].shape[0]
    out = jnp.zeros((size * len(parts),) + parts[0].shape[1:], parts[0].dtype)
    for k, part in enumerate(parts):
        out = lax.dynamic_update_slice_in_dim(out, part, (me ^ k) * size, 0)
    return out


def halves(x):
    high = lax.reduce_precision(x, 8, 7)
    return high.astype(BF16), (x - high).astype(BF16)


def joined(x):
    size = x.shape[0] // 2
    return x[:size].astype(F32) + x[size:].astype(F32)


def edges(rows):
    count = lax.axis_size("rows")
    even = lax.axis_index("rows") % 2 == 0
    first, last = rows[:3], rows[-3:]
    a = exchange(jnp.where(even, last, first), "rows", 1)
    pairs = [(i, i + 1) for i in range(1, count - 1, 2)]
    b = lax.ppermute(jnp.where(even, first, last), "rows", pairs + [(j, i) for i, j in pairs])
    return jnp.where(even, b, a), jnp.where(even, a, b)


def on_device(
    features,
    depth_kernel,
    depth_bias,
    norm_gain,
    norm_bias,
    up_weight,
    up_bias,
    down_weight,
    down_bias,
    layer_scale,
    tissue,
    aggregator_order,
    tile_cotangent,
):
    channels, height, across = features.shape[1:]
    hidden_units = up_weight.shape[1]
    row_count = lax.axis_size("rows")
    tiles_here = across // TILE
    scale = 1.0 / math.sqrt(lax.axis_size("slide") * row_count * height * across)

    sent = jnp.broadcast_to(tile_cotangent, (row_count,) + tile_cotangent.shape[1:])
    first_rows = features[0, :, :3].transpose(1, 0, 2)
    last_rows = features[0, :, -3:].transpose(1, 0, 2)
    top, bottom = edges(jnp.concatenate([first_rows, last_rows], axis=0))
    image = features[0].transpose(1, 0, 2)
    image_shape = (height, channels, across)
    vectors = jnp.stack([depth_bias, norm_gain, norm_bias], axis=1)
    spread = pltpu.VMEM((49, 8, LANES), F32)
    cotangents = lax.all_to_all(sent, "rows", 0, 0, tiled=True).reshape(-1, channels)
    convolved, feature_sum = call(
        forward_kernel,
        [whole(x) for x in (top, image, bottom, depth_kernel, vectors)],
        [(image_shape, F32), ((channels, across), F32)],
        [pltpu.VMEM((height + 6, channels, across), F32), spread],
        CONV_COST,
        "convolution",
        CONV_MIB,
    )
    me = lax.axis_index("rows")
    positions = lax.dynamic_slice_in_dim(aggregator_order[0], me * tiles_here, tiles_here)
    meta = jnp.pad(jnp.stack([positions, tissue[0, 0]], axis=1), ((0, 8 - tiles_here), (0, 0)))
    row_vectors = jnp.stack([layer_scale, down_bias], axis=0)

    part_rows = 2 * channels * hidden_units // LANES
    operands = (
        convolved, feature_sum, cotangents, meta, vectors, row_vectors,
        up_weight, up_weight.T, down_weight, up_bias[:, None],
    )
    grad_conv, part, embedding, cotangent = call(
        functools.partial(mlp_kernel, scale=scale),
        [whole(x) for x in operands],
        [(image_shape, BF16), ((part_rows, LANES), F32), ((8, channels), F32), ((channels, across), F32)],
        [
            pltpu.VMEM((2, hidden_units, 2 * LANES), F32),
            pltpu.VMEM((2, hidden_units, 2 * LANES), BF16),
            pltpu.VMEM((hidden_units, LANES), F32),
            pltpu.VMEM((hidden_units, LANES), F32),
            pltpu.VMEM((hidden_units, LANES), F32),
            pltpu.VMEM((channels, hidden_units), F32),
            pltpu.VMEM((2, channels, LANES), F32),
            pltpu.VMEM((2, channels, 2 * LANES), BF16),
            pltpu.VMEM((2, 2, channels, LANES), F32),
            pltpu.VMEM((2, 2, LANES), F32),
        ],
        25,
        "mlp_both_ways",
    )

    grad_top, grad_bottom = edges(grad_conv)
    quarter = channels // 4
    wide = pltpu.VMEM((height + 6, quarter, across), F32)

    def kernel_piece(k, *gates):
        grad = after([grad_conv], *gates)[0]
        operands = [part_of(x, 1, quarter, k) for x in (top, image, bottom, grad)]
        return call(
            functools.partial(kernel_grad_kernel, scale=scale, lane0=LANES // 2 * (k // 2)),
            operands,
            [((quarter, LANES), F32)],
            [wide, pltpu.VMEM((height, quarter, across), F32), spread],
            4,
            "kernel_grad",
        )[0]

    def input_piece(k, *gates):
        grad = after([grad_conv], *gates)[0]
        operands = [part_of(x, 1, quarter, k) for x in (grad_top, grad, grad_bottom)]
        return call(
            input_grad_kernel,
            operands + [part_of(x, 0, quarter, k) for x in (depth_kernel, cotangent)],
            [((quarter * height, across), BF16)],
            [wide, spread, pltpu.VMEM((8 * height, across), F32)],
            4,
            "input_grad",
        )[0]

    terms = [kernel_piece(0)]
    own = tree(after(send_parts(part, "slide", (1,)), terms[0]))
    terms.append(kernel_piece(1, own))
    terms.append(kernel_piece(2, own))
    own = tree(after(send_parts(own, "rows", (1, 2)), *terms))
    terms.append(kernel_piece(3, own, grad_top, grad_bottom))
    own = tree(after(send_parts(own, "rows", (8, 16)), *terms))
    size = own.shape[0]
    taps = jnp.concatenate([terms[0] + terms[2], terms[1] + terms[3]], axis=0)
    own = jnp.concatenate([own, taps], axis=0)
    grads = [input_piece(0, own)]
    own = tree(after(send_all(own, "rows", (4, 32)), grads[0]))
    grads.append(input_piece(1, own))
    own = tree(after(send_all(own, "slide", (2,)), grads[1]))
    grads.append(input_piece(2, own))
    parts = after(send_all(own, "rows", (8, 16)), grads[2])
    taps = tree([x[size:] for x in parts])
    own = in_order([x[:size] for x in parts], "rows", (8, 16)).astype(BF16)
    size = 4 * size
    own = jnp.concatenate([own, *halves(taps)], axis=0)
    grads.append(input_piece(3, own))
    parts = after(send_all(own, "rows", (1, 2)), grads[3])
    taps = tree([joined(x[size:]) for x in parts])
    own = in_order([x[:size] for x in parts], "rows", (1, 2))
    size = 4 * size
    own = jnp.concatenate([own, *halves(taps)], axis=0)
    there = exchange(own, "slide", 1)
    low = rank_in("slide", (1,)) == 0
    first = jnp.where(low, own[:size], there[:size]).astype(F32)
    second = jnp.where(low, there[:size], own[:size]).astype(F32)
    taps = joined(own[size:]) + joined(there[size:])

    def untile(x):
        tiled = x.reshape(channels // 8, hidden_units // LANES, 8, LANES)
        return tiled.transpose(0, 2, 1, 3).reshape(channels, hidden_units)

    grad_kernel = jnp.concatenate([taps[:, :49], taps[:, LANES // 2 : LANES // 2 + 49]], axis=0)
    input_grad = jnp.concatenate(grads, axis=0).reshape((1, channels, height, across))
    return (embedding[None, :tiles_here], input_grad, untile(first), untile(second).T, grad_kernel)


def solution(mesh):
    return jax.shard_map(
        on_device,
        mesh=mesh,
        in_specs=(
            P("slide", None, "rows", None),
            P(),
            P(),
            P(),
            P(),
            P(),
            P(),
            P(),
            P(),
            P(),
            P("slide", "rows", None),
            P("slide", None),
            P("slide", "rows", None),
        ),
        out_specs=(P("slide", "rows", None), P("slide", None, "rows", None), P(), P(), P()),
        check_vma=False,
    )
```

```python
import functools
import math

import jax
import jax.numpy as jnp
from jax import lax
from jax.experimental import pallas as pl
from jax.experimental.pallas import tpu as pltpu
from jax.sharding import PartitionSpec as P

TILE = 32
LANES = 128
HIGHEST = lax.Precision.HIGHEST
F32 = jnp.float32
BF16 = jnp.bfloat16


def lane_ids(rows):
    return lax.broadcasted_iota(jnp.int32, (rows, LANES), 1)


def spread_taps(taps, spread_ref, flip):
    lanes = lane_ids(8)
    for a in range(7):
        for b in range(7):
            tap = 7 * (6 - a) + (6 - b) if flip else 7 * a + b
            value = jnp.broadcast_to(taps[:, tap : tap + 1], (8, LANES))
            shift = b - 3
            if shift > 0:
                value = jnp.where(lanes >= shift, value, 0.0)
            elif shift < 0:
                value = jnp.where(lanes < LANES + shift, value, 0.0)
            spread_ref[7 * a + b] = value


def depthwise(source_ref, spread_ref, c0, store, height):
    step = 16
    for first in range(0, height, step):
        rows = [source_ref[first + r, pl.ds(c0, 8), :] for r in range(step + 6)]
        sums = [None] * step
        for b in range(7):
            taps = [spread_ref[7 * a + b] for a in range(7)]
            for i in range(step):
                part = taps[0] * rows[i]
                for a in range(1, 7):
                    part = part + taps[a] * rows[i + a]
                if b != 3:
                    part = pltpu.roll(part, (3 - b) % LANES, 1)
                sums[i] = part if b == 0 else sums[i] + part
        for i in range(step):
            store(first + i, sums[i])


def widen(top_ref, mid_ref, bottom_ref, wide_ref):
    height = mid_ref.shape[0]
    for r in range(3):
        wide_ref[r] = top_ref[r].astype(F32)
        wide_ref[height + 3 + r] = bottom_ref[r].astype(F32)

    def copy(r, carry):
        wide_ref[r + 3] = mid_ref[r].astype(F32)
        return carry

    lax.fori_loop(0, height, copy, 0)


def forward_kernel(
    top_ref, mid_ref, bottom_ref, taps_ref, vectors_ref, out_ref, feature_sum_ref, wide_ref, spread_ref
):
    height, channels, _ = mid_ref.shape
    widen(top_ref, mid_ref, bottom_ref, wide_ref)

    def conv(block, carry):
        c0 = pl.multiple_of(block * 8, 8)
        spread_taps(taps_ref[pl.ds(c0, 8), :], spread_ref, False)
        bias = jnp.broadcast_to(vectors_ref[pl.ds(c0, 8), 0:1], (8, LANES))

        def store(i, value):
            out_ref[i, pl.ds(c0, 8), :] = value + bias

        depthwise(wide_ref, spread_ref, c0, store, height)
        total = wide_ref[3, pl.ds(c0, 8), :]
        for i in range(1, height):
            total = total + wide_ref[3 + i, pl.ds(c0, 8), :]
        feature_sum_ref[pl.ds(c0, 8), :] = total
        return carry

    lax.fori_loop(0, channels // 8, conv, 0)


def gelu_parts(v):
    cumulative = 0.5 + 0.5 * lax.erf(v * 0.7071067811865476)
    density = jnp.exp(v * v * -0.5)
    return v * cumulative, cumulative + v * (density * 0.3989422804014327)


def mlp_kernel(
    conv_a_ref, conv_b_ref, sum_a_ref, sum_b_ref, gathered_ref, meta_ref, vectors_ref, row_vectors_ref,
    up_ref, up_t_ref, down_ref, up_bias_ref,
    grad_conv_ref, part_ref, embedding_ref, cotangent_ref,
    pre_ref, grad_ref, slope_scale_ref, bias_ref, hidden_sum_ref, up_sum_ref, gain_ref,
    normed_ref, standard_ref, reciprocal_ref,
    *, scale,
):
    height = conv_a_ref.shape[0]
    channels = vectors_ref.shape[0]
    hidden_units = down_ref.shape[0]
    tiles = gathered_ref.shape[0]
    picks = lax.broadcasted_iota(jnp.int32, (8, tiles), 1) == meta_ref[:, 0:1]
    wanted = jnp.dot(picks.astype(BF16), gathered_ref[...], preferred_element_type=F32)
    mask = meta_ref[:, 1:2].astype(F32)
    scaled_mask = mask * row_vectors_ref[0:1, :]
    branch_rows = (scaled_mask * wanted).astype(BF16)
    member = lax.broadcasted_iota(jnp.int32, (8, LANES), 1) // TILE == lax.broadcasted_iota(
        jnp.int32, (8, LANES), 0
    )
    member_f32 = member.astype(F32)
    first = (((0,), (0,)), ((), ()))
    last = (((1,), (1,)), ((), ()))
    grad_branch = lax.dot_general(
        branch_rows.astype(F32), member_f32, first, precision=HIGHEST, preferred_element_type=F32
    ).astype(BF16)
    cotangent_ref[...] = lax.dot_general(
        wanted, member_f32, first, precision=HIGHEST, preferred_element_type=F32
    )
    slope_scale_ref[...] = jnp.dot(down_ref[...], grad_branch, preferred_element_type=F32)
    bias_ref[...] = jnp.broadcast_to(up_bias_ref[...], (hidden_units, LANES))
    gain_ref[0] = jnp.broadcast_to(vectors_ref[:, 1:2], (channels, LANES))
    gain_ref[1] = jnp.broadcast_to(vectors_ref[:, 2:3], (channels, LANES))
    hidden_sum_ref[...] = jnp.zeros_like(hidden_sum_ref)
    up_sum_ref[...] = jnp.zeros_like(up_sum_ref)
    chunk = 256
    step = 2

    blocks = height // step

    def norm(block, slot):
        for r in range(step):
            row = block * step + r
            values = jnp.concatenate([conv_a_ref[row], conv_b_ref[row]], axis=0)
            average = jnp.sum(values, axis=0, keepdims=True) * (1.0 / channels)
            centered = values - average
            variance = jnp.sum(centered * centered, axis=0, keepdims=True) * (1.0 / channels)
            reciprocal = lax.rsqrt(variance + 1e-06)
            standard = centered * reciprocal
            standard_ref[slot, r] = standard
            reciprocal_ref[slot, r : r + 1, :] = reciprocal
            normed_ref[slot, :, r * LANES : (r + 1) * LANES] = (standard * gain_ref[0] + gain_ref[1]).astype(BF16)

    def enter(slot, f0, normed):
        pre_ref[slot, f0 : f0 + chunk, :] = jnp.dot(
            up_t_ref[f0 : f0 + chunk, :], normed, preferred_element_type=F32
        )

    def leave(block, slot, following):
        r0 = block * step
        normed = normed_ref[slot]
        norm(following, 1 - slot)
        after = normed_ref[1 - slot]
        grad_normed = None
        for f0 in range(0, hidden_units, chunk):
            enter(1 - slot, f0, after)
            for f in range(f0, f0 + chunk, 16):
                total = hidden_sum_ref[f : f + 16, :]
                for r in range(step):
                    cols = slice(r * LANES, (r + 1) * LANES)
                    hidden, slope = gelu_parts(pre_ref[slot, f : f + 16, cols] + bias_ref[f : f + 16, :])
                    total = total + hidden
                    grad_ref[slot, f : f + 16, cols] = (slope_scale_ref[f : f + 16, :] * slope).astype(BF16)
                hidden_sum_ref[f : f + 16, :] = total
            grad = grad_ref[slot, f0 : f0 + chunk, :]
            term = jnp.dot(up_ref[:, f0 : f0 + chunk], grad, preferred_element_type=F32)
            grad_normed = term if grad_normed is None else grad_normed + term
            up_sum_ref[:, f0 : f0 + chunk] += lax.dot_general(
                normed, grad, last, preferred_element_type=F32
            )
        for r in range(step):
            grad_standard = grad_normed[:, r * LANES : (r + 1) * LANES] * gain_ref[0]
            standard = standard_ref[slot, r]
            m1 = jnp.sum(grad_standard, axis=0, keepdims=True) * (1.0 / channels)
            m2 = jnp.sum(grad_standard * standard, axis=0, keepdims=True) * (1.0 / channels)
            grad_conv_ref[r0 + r] = (
                reciprocal_ref[slot, r : r + 1, :] * (grad_standard - m1 - standard * m2)
            ).astype(BF16)

    norm(0, 0)
    start = normed_ref[0]
    for f0 in range(0, hidden_units, chunk):
        enter(0, f0, start)

    def pair(k, carry):
        leave(2 * k, 0, 2 * k + 1)
        leave(2 * k + 1, 1, jnp.minimum(2 * k + 2, blocks - 1))
        return carry

    lax.fori_loop(0, blocks // 2, pair, 0)
    hidden_rows = lax.dot_general(
        member_f32, hidden_sum_ref[...], last, precision=HIGHEST, preferred_element_type=F32
    )
    inverse = 1.0 / (height * TILE)
    branch = jnp.dot(
        hidden_rows * inverse, down_ref[...].astype(F32), precision=HIGHEST, preferred_element_type=F32
    ) + row_vectors_ref[1:2, :]
    features = lax.dot_general(
        member_f32, jnp.concatenate([sum_a_ref[...], sum_b_ref[...]], axis=0), last, precision=HIGHEST, preferred_element_type=F32
    )
    embedding_ref[...] = features * inverse + scaled_mask * branch
    down_sum = lax.dot_general(
        branch_rows.astype(F32), hidden_rows * scale, first, precision=HIGHEST, preferred_element_type=F32
    )
    across = hidden_units // LANES
    half = (channels // 8) * across
    for r in range(channels // 8):
        for k in range(across):
            at = (r * across + k) * 8
            cols = slice(k * LANES, (k + 1) * LANES)
            part_ref[at : at + 8, :] = up_sum_ref[8 * r : 8 * r + 8, cols] * scale
            part_ref[half * 8 + at : half * 8 + at + 8, :] = down_sum[8 * r : 8 * r + 8, cols]


def kernel_grad_kernel(
    top_ref, mid_ref, bottom_ref, grad_ref, out_ref, wide_ref, wide_grad_ref, tiles_ref, *, scale, lane0
):
    height, channels, _ = mid_ref.shape
    widen(top_ref, mid_ref, bottom_ref, wide_ref)

    def copy(r, carry):
        wide_grad_ref[r] = grad_ref[r].astype(F32)
        return carry

    lax.fori_loop(0, height, copy, 0)
    lanes = lane_ids(8)

    def conv(block, carry):
        c0 = pl.multiple_of(block * 8, 8)
        for b in range(7):
            shift = b - 3
            sums = [None] * 7
            for i in range(height):
                grad = wide_grad_ref[i, pl.ds(c0, 8), :]
                if shift != 0:
                    grad = pltpu.roll(grad, shift % LANES, 1)
                for a in range(7):
                    term = grad * wide_ref[i + a, pl.ds(c0, 8), :]
                    sums[a] = term if i == 0 else sums[a] + term
            for a in range(7):
                tiles_ref[7 * a + b] = sums[a]
        out = jnp.zeros((8, LANES), F32)
        for tap in range(49):
            shift = tap % 7 - 3
            total = tiles_ref[tap]
            if shift > 0:
                total = jnp.where(lanes >= shift, total, 0.0)
            elif shift < 0:
                total = jnp.where(lanes < LANES + shift, total, 0.0)
            total = jnp.sum(total, axis=1, keepdims=True)
            out = jnp.where(lanes == lane0 + tap, total, out)
        out_ref[pl.ds(c0, 8), :] = out * scale
        return carry

    lax.fori_loop(0, channels // 8, conv, 0)


def input_grad_kernel(
    top_ref, mid_ref, bottom_ref, taps_ref, cotangent_ref, out_ref, wide_ref, spread_ref, sum_ref
):
    height, channels, _ = mid_ref.shape
    widen(top_ref, mid_ref, bottom_ref, wide_ref)

    def conv(block, carry):
        c0 = pl.multiple_of(block * 8, 8)
        spread_taps(taps_ref[pl.ds(c0, 8), :], spread_ref, True)
        cotangent = cotangent_ref[pl.ds(c0, 8), :]

        def store(i, value):
            sum_ref[pl.ds(i, 8, stride=height), :] = value + cotangent

        depthwise(wide_ref, spread_ref, c0, store, height)
        at = pl.multiple_of(c0 * height, 8 * height)
        out_ref[pl.ds(at, 8 * height), :] = sum_ref[...].astype(BF16)
        return carry

    lax.fori_loop(0, channels // 8, conv, 0)


CONV_MIB = 58


def cost(us):
    return pl.CostEstimate(flops=int(us * 1.0e9), bytes_accessed=1 << 20, transcendentals=0)


def whole(x):
    return (x, x.shape, None, 0)


def part_of(x, dim, size, k):
    return (x, tuple(size if d == dim else n for d, n in enumerate(x.shape)), dim, k)


def call(kernel, operands, shapes, scratch, us, name, mib=40):
    def spec(shape, dim=None, k=0):
        return pl.BlockSpec(shape, lambda i: tuple(k if d == dim else 0 for d in range(len(shape))))

    return pl.pallas_call(
        kernel,
        grid=(1,),
        in_specs=[spec(*operand[1:]) for operand in operands],
        out_specs=[spec(shape) for shape, _ in shapes],
        out_shape=[jax.ShapeDtypeStruct(*shape) for shape in shapes],
        scratch_shapes=scratch,
        compiler_params=pltpu.CompilerParams(vmem_limit_bytes=mib << 20),
        cost_estimate=cost(us),
        name=name,
    )(*[operand[0] for operand in operands])


def after(xs, *others):
    return lax.optimization_barrier((tuple(xs), others))[0]


def patterns(bits):
    return [sum(bit for k, bit in enumerate(bits) if (p >> k) & 1) for p in range(1, 1 << len(bits))]


def exchange(x, axis, pattern):
    return lax.ppermute(x, axis, [(i, i ^ pattern) for i in range(lax.axis_size(axis))])


def rank_in(axis, bits):
    index = lax.axis_index(axis)
    return sum(((index // bit) % 2) * (1 << k) for k, bit in enumerate(bits))


def run(x, k, count):
    size = x.shape[0] // count
    return lax.dynamic_slice_in_dim(x, k * size, size)


def tree(parts):
    while len(parts) > 1:
        parts = [parts[k] + parts[k + 1] for k in range(0, len(parts), 2)]
    return parts[0]


def send_parts(x, axis, bits):
    me = rank_in(axis, bits)
    count = 1 << len(bits)
    sent = [exchange(run(x, me ^ (k + 1), count), axis, p) for k, p in enumerate(patterns(bits))]
    return [run(x, me, count)] + sent


def send_all(x, axis, bits):
    return [x] + [exchange(x, axis, p) for p in patterns(bits)]


def in_order(parts, axis, bits):
    me = rank_in(axis, bits)
    size = parts[0].shape[0]
    out = jnp.zeros((size * len(parts),) + parts[0].shape[1:], parts[0].dtype)
    for k, part in enumerate(parts):
        out = lax.dynamic_update_slice_in_dim(out, part, (me ^ k) * size, 0)
    return out


def share(x, bits):
    ways = [0] + patterns(bits)
    groups = [[i ^ p for p in ways] for i in range(lax.axis_size("rows")) if i & sum(bits) == 0]
    sent = jnp.broadcast_to(x, (len(ways),) + x.shape)
    return lax.all_to_all(sent, "rows", 0, 0, axis_index_groups=groups, tiled=True)


def halves(x):
    high = lax.reduce_precision(x, 8, 7)
    return high.astype(BF16), (x - high).astype(BF16)


def joined(x):
    size = x.shape[0] // 2
    return x[:size].astype(F32) + x[size:].astype(F32)


def edges(rows):
    count = lax.axis_size("rows")
    even = lax.axis_index("rows") % 2 == 0
    first, last = rows[:3], rows[-3:]
    a = exchange(jnp.where(even, last, first), "rows", 1)
    pairs = [(i, i + 1) for i in range(1, count - 1, 2)]
    b = lax.ppermute(jnp.where(even, first, last), "rows", pairs + [(j, i) for i, j in pairs])
    return jnp.where(even, b, a), jnp.where(even, a, b)


def on_device(
    features,
    depth_kernel,
    depth_bias,
    norm_gain,
    norm_bias,
    up_weight,
    up_bias,
    down_weight,
    down_bias,
    layer_scale,
    tissue,
    aggregator_order,
    tile_cotangent,
):
    channels, height, across = features.shape[1:]
    hidden_units = up_weight.shape[1]
    row_count = lax.axis_size("rows")
    tiles_here = across // TILE
    scale = 1.0 / math.sqrt(lax.axis_size("slide") * row_count * height * across)

    first_rows = features[0, :, :3].transpose(1, 0, 2)
    last_rows = features[0, :, -3:].transpose(1, 0, 2)
    top, bottom = edges(jnp.concatenate([first_rows, last_rows], axis=0))
    image = features[0].transpose(1, 0, 2)
    image_shape = (height, channels, across)
    vectors = jnp.stack([depth_bias, norm_gain, norm_bias], axis=1)
    spread = pltpu.VMEM((49, 8, LANES), F32)
    half = channels // 2
    cotangents = tile_cotangent[0]
    convolved = []
    feature_sums = []
    for k, bits in enumerate(((1, 2, 4), (8, 16, 32))):
        gathered = share(cotangents, bits)
        source = after([image], cotangents, *convolved)[0]
        operands = [part_of(x, 1, half, k) for x in (top, source, bottom)]
        out, total = call(
            forward_kernel,
            operands + [part_of(depth_kernel, 0, half, k), part_of(vectors, 0, half, k)],
            [((height, half, across), F32), ((half, across), F32)],
            [pltpu.VMEM((height + 6, half, across), F32), spread],
            8,
            "convolution",
            CONV_MIB,
        )
        convolved.append(out)
        feature_sums.append(total)
        cotangents = after([gathered], out)[0].reshape(-1, channels)
    me = lax.axis_index("rows")
    positions = lax.dynamic_slice_in_dim(aggregator_order[0], me * tiles_here, tiles_here)
    meta = jnp.pad(jnp.stack([positions, tissue[0, 0]], axis=1), ((0, 8 - tiles_here), (0, 0)))
    row_vectors = jnp.stack([layer_scale, down_bias], axis=0)

    part_rows = 2 * channels * hidden_units // LANES
    operands = (
        *convolved, *feature_sums, cotangents, meta, vectors, row_vectors,
        up_weight, up_weight.T, down_weight, up_bias[:, None],
    )
    grad_conv, part, embedding, cotangent = call(
        functools.partial(mlp_kernel, scale=scale),
        [whole(x) for x in operands],
        [(image_shape, BF16), ((part_rows, LANES), F32), ((8, channels), F32), ((channels, across), F32)],
        [
            pltpu.VMEM((2, hidden_units, 2 * LANES), F32),
            pltpu.VMEM((2, hidden_units, 2 * LANES), BF16),
            pltpu.VMEM((hidden_units, LANES), F32),
            pltpu.VMEM((hidden_units, LANES), F32),
            pltpu.VMEM((hidden_units, LANES), F32),
            pltpu.VMEM((channels, hidden_units), F32),
            pltpu.VMEM((2, channels, LANES), F32),
            pltpu.VMEM((2, channels, 2 * LANES), BF16),
            pltpu.VMEM((2, 2, channels, LANES), F32),
            pltpu.VMEM((2, 2, LANES), F32),
        ],
        25,
        "mlp_both_ways",
    )

    grad_top, grad_bottom = edges(grad_conv)
    quarter = channels // 4
    wide = pltpu.VMEM((height + 6, quarter, across), F32)

    def kernel_piece(k, *gates):
        grad = after([grad_conv], *gates)[0]
        operands = [part_of(x, 1, quarter, k) for x in (top, image, bottom, grad)]
        return call(
            functools.partial(kernel_grad_kernel, scale=scale, lane0=LANES // 2 * (k // 2)),
            operands,
            [((quarter, LANES), F32)],
            [wide, pltpu.VMEM((height, quarter, across), F32), spread],
            4,
            "kernel_grad",
        )[0]

    def input_piece(k, *gates):
        grad = after([grad_conv], *gates)[0]
        operands = [part_of(x, 1, quarter, k) for x in (grad_top, grad, grad_bottom)]
        return call(
            input_grad_kernel,
            operands + [part_of(x, 0, quarter, k) for x in (depth_kernel, cotangent)],
            [((quarter * height, across), BF16)],
            [wide, spread, pltpu.VMEM((8 * height, across), F32)],
            4,
            "input_grad",
        )[0]

    terms = [kernel_piece(0)]
    part = after([part], grad_top, grad_bottom, terms[0])[0]
    terms.append(kernel_piece(1, grad_top, grad_bottom, terms[0]))
    own = tree(after(send_parts(part, "slide", (1,)), terms[1]))
    terms.append(kernel_piece(2, own))
    own = tree(after(send_parts(own, "rows", (1, 2)), terms[2]))
    terms.append(kernel_piece(3, own))
    own = tree(after(send_parts(own, "rows", (8, 16)), terms[3]))
    size = own.shape[0]
    taps = jnp.concatenate([terms[0] + terms[2], terms[1] + terms[3]], axis=0)
    own = jnp.concatenate([own, taps], axis=0)
    grads = []
    for axis, bit in (("rows", 32), ("rows", 4), ("slide", 2)):
        grads.append(input_piece(len(grads), own))
        own = tree(after(send_all(own, axis, (bit,)), grads[-1]))
    grads.append(input_piece(3, own))
    parts = after(send_all(own, "rows", (8, 16)), grads[3])
    taps = tree([x[size:] for x in parts])
    own = in_order([x[:size] for x in parts], "rows", (8, 16)).astype(BF16)
    size = 4 * size
    own = jnp.concatenate([own, *halves(taps)], axis=0)
    parts = send_all(own, "rows", (1, 2))
    taps = tree([joined(x[size:]) for x in parts])
    own = in_order([x[:size] for x in parts], "rows", (1, 2))
    size = 4 * size
    own = jnp.concatenate([own, *halves(taps)], axis=0)
    there = exchange(own, "slide", 1)
    low = rank_in("slide", (1,)) == 0
    first = jnp.where(low, own[:size], there[:size]).astype(F32)
    second = jnp.where(low, there[:size], own[:size]).astype(F32)
    taps = joined(own[size:]) + joined(there[size:])

    def untile(x):
        tiled = x.reshape(channels // 8, hidden_units // LANES, 8, LANES)
        return tiled.transpose(0, 2, 1, 3).reshape(channels, hidden_units)

    grad_kernel = jnp.concatenate([taps[:, :49], taps[:, LANES // 2 : LANES // 2 + 49]], axis=0)
    input_grad = jnp.concatenate(grads, axis=0).reshape((1, channels, height, across))
    return (embedding[None, :tiles_here], input_grad, untile(first), untile(second).T, grad_kernel)


def solution(mesh):
    return jax.shard_map(
        on_device,
        mesh=mesh,
        in_specs=(
            P("slide", None, "rows", None),
            P(),
            P(),
            P(),
            P(),
            P(),
            P(),
            P(),
            P(),
            P(),
            P("slide", "rows", None),
            P("slide", None),
            P("slide", "rows", None),
        ),
        out_specs=(P("slide", "rows", None), P("slide", None, "rows", None), P(), P(), P()),
        check_vma=False,
    )
```

```python
import functools
import math

import jax
import jax.numpy as jnp
from jax import lax
from jax.experimental import pallas as pl
from jax.experimental.pallas import tpu as pltpu
from jax.sharding import PartitionSpec as P

TILE = 32
LANES = 128
HIGHEST = lax.Precision.HIGHEST
F32 = jnp.float32
BF16 = jnp.bfloat16


def lane_ids(rows):
    return lax.broadcasted_iota(jnp.int32, (rows, LANES), 1)


def spread_taps(taps, spread_ref, flip):
    lanes = lane_ids(8)
    for a in range(7):
        for b in range(7):
            tap = 7 * (6 - a) + (6 - b) if flip else 7 * a + b
            value = jnp.broadcast_to(taps[:, tap : tap + 1], (8, LANES))
            shift = b - 3
            if shift > 0:
                value = jnp.where(lanes >= shift, value, 0.0)
            elif shift < 0:
                value = jnp.where(lanes < LANES + shift, value, 0.0)
            spread_ref[7 * a + b] = value


def depthwise(source_ref, spread_ref, c0, store, height):
    step = 16
    for first in range(0, height, step):
        rows = [source_ref[first + r, pl.ds(c0, 8), :] for r in range(step + 6)]
        sums = [None] * step
        for b in range(7):
            taps = [spread_ref[7 * a + b] for a in range(7)]
            for i in range(step):
                part = taps[0] * rows[i]
                for a in range(1, 7):
                    part = part + taps[a] * rows[i + a]
                if b != 3:
                    part = pltpu.roll(part, (3 - b) % LANES, 1)
                sums[i] = part if b == 0 else sums[i] + part
        for i in range(step):
            store(first + i, sums[i])


def widen(top_ref, mid_ref, bottom_ref, wide_ref):
    height = mid_ref.shape[0]
    for r in range(3):
        wide_ref[r] = top_ref[r].astype(F32)
        wide_ref[height + 3 + r] = bottom_ref[r].astype(F32)

    def copy(r, carry):
        wide_ref[r + 3] = mid_ref[r].astype(F32)
        return carry

    lax.fori_loop(0, height, copy, 0)


def forward_kernel(
    top_ref, mid_ref, bottom_ref, taps_ref, vectors_ref, out_ref, feature_sum_ref, wide_ref, spread_ref
):
    height, channels, _ = mid_ref.shape
    widen(top_ref, mid_ref, bottom_ref, wide_ref)

    def conv(block, carry):
        c0 = pl.multiple_of(block * 8, 8)
        spread_taps(taps_ref[pl.ds(c0, 8), :], spread_ref, False)
        bias = jnp.broadcast_to(vectors_ref[pl.ds(c0, 8), 0:1], (8, LANES))

        def store(i, value):
            out_ref[i, pl.ds(c0, 8), :] = value + bias

        depthwise(wide_ref, spread_ref, c0, store, height)
        total = wide_ref[3, pl.ds(c0, 8), :]
        for i in range(1, height):
            total = total + wide_ref[3 + i, pl.ds(c0, 8), :]
        feature_sum_ref[pl.ds(c0, 8), :] = total
        return carry

    lax.fori_loop(0, channels // 8, conv, 0)


def gelu_parts(v):
    cumulative = 0.5 + 0.5 * lax.erf(v * 0.7071067811865476)
    density = jnp.exp(v * v * -0.5)
    return v * cumulative, cumulative + v * (density * 0.3989422804014327)


def mlp_kernel(
    conv_ref, feature_sum_ref, gathered_ref, meta_ref, vectors_ref, row_vectors_ref,
    up_ref, up_t_ref, down_ref, up_bias_ref,
    grad_conv_ref, part_ref, embedding_ref, cotangent_ref,
    pre_ref, grad_ref, slope_scale_ref, bias_ref, hidden_sum_ref, up_sum_ref, gain_ref,
    normed_ref, standard_ref, reciprocal_ref,
    *, scale,
):
    height = conv_ref.shape[0]
    channels = vectors_ref.shape[0]
    hidden_units = down_ref.shape[0]
    tiles = gathered_ref.shape[0]
    picks = lax.broadcasted_iota(jnp.int32, (8, tiles), 1) == meta_ref[:, 0:1]
    wanted = jnp.dot(picks.astype(BF16), gathered_ref[...], preferred_element_type=F32)
    mask = meta_ref[:, 1:2].astype(F32)
    scaled_mask = mask * row_vectors_ref[0:1, :]
    branch_rows = (scaled_mask * wanted).astype(BF16)
    member = lax.broadcasted_iota(jnp.int32, (8, LANES), 1) // TILE == lax.broadcasted_iota(
        jnp.int32, (8, LANES), 0
    )
    member_f32 = member.astype(F32)
    first = (((0,), (0,)), ((), ()))
    last = (((1,), (1,)), ((), ()))
    grad_branch = lax.dot_general(
        branch_rows.astype(F32), member_f32, first, precision=HIGHEST, preferred_element_type=F32
    ).astype(BF16)
    cotangent_ref[...] = lax.dot_general(
        wanted, member_f32, first, precision=HIGHEST, preferred_element_type=F32
    )
    slope_scale_ref[...] = jnp.dot(down_ref[...], grad_branch, preferred_element_type=F32)
    bias_ref[...] = jnp.broadcast_to(up_bias_ref[...], (hidden_units, LANES))
    gain_ref[0] = jnp.broadcast_to(vectors_ref[:, 1:2], (channels, LANES))
    gain_ref[1] = jnp.broadcast_to(vectors_ref[:, 2:3], (channels, LANES))
    hidden_sum_ref[...] = jnp.zeros_like(hidden_sum_ref)
    up_sum_ref[...] = jnp.zeros_like(up_sum_ref)
    chunk = 256
    step = 2

    blocks = height // step

    def norm(block, slot):
        for r in range(step):
            row = block * step + r
            values = conv_ref[row]
            average = jnp.sum(values, axis=0, keepdims=True) * (1.0 / channels)
            centered = values - average
            variance = jnp.sum(centered * centered, axis=0, keepdims=True) * (1.0 / channels)
            reciprocal = lax.rsqrt(variance + 1e-06)
            standard = centered * reciprocal
            standard_ref[slot, r] = standard
            reciprocal_ref[slot, r : r + 1, :] = reciprocal
            normed_ref[slot, :, r * LANES : (r + 1) * LANES] = (standard * gain_ref[0] + gain_ref[1]).astype(BF16)

    def enter(slot, f0, normed):
        pre_ref[slot, f0 : f0 + chunk, :] = jnp.dot(
            up_t_ref[f0 : f0 + chunk, :], normed, preferred_element_type=F32
        )

    def leave(block, slot, following):
        r0 = block * step
        normed = normed_ref[slot]
        norm(following, 1 - slot)
        after = normed_ref[1 - slot]
        grad_normed = None
        for f0 in range(0, hidden_units, chunk):
            enter(1 - slot, f0, after)
            for f in range(f0, f0 + chunk, 16):
                total = hidden_sum_ref[f : f + 16, :]
                for r in range(step):
                    cols = slice(r * LANES, (r + 1) * LANES)
                    hidden, slope = gelu_parts(pre_ref[slot, f : f + 16, cols] + bias_ref[f : f + 16, :])
                    total = total + hidden
                    grad_ref[slot, f : f + 16, cols] = (slope_scale_ref[f : f + 16, :] * slope).astype(BF16)
                hidden_sum_ref[f : f + 16, :] = total
            grad = grad_ref[slot, f0 : f0 + chunk, :]
            term = jnp.dot(up_ref[:, f0 : f0 + chunk], grad, preferred_element_type=F32)
            grad_normed = term if grad_normed is None else grad_normed + term
            up_sum_ref[:, f0 : f0 + chunk] += lax.dot_general(
                normed, grad, last, preferred_element_type=F32
            )
        for r in range(step):
            grad_standard = grad_normed[:, r * LANES : (r + 1) * LANES] * gain_ref[0]
            standard = standard_ref[slot, r]
            m1 = jnp.sum(grad_standard, axis=0, keepdims=True) * (1.0 / channels)
            m2 = jnp.sum(grad_standard * standard, axis=0, keepdims=True) * (1.0 / channels)
            grad_conv_ref[r0 + r] = (
                reciprocal_ref[slot, r : r + 1, :] * (grad_standard - m1 - standard * m2)
            ).astype(BF16)

    norm(0, 0)
    start = normed_ref[0]
    for f0 in range(0, hidden_units, chunk):
        enter(0, f0, start)

    def pair(k, carry):
        leave(2 * k, 0, 2 * k + 1)
        leave(2 * k + 1, 1, jnp.minimum(2 * k + 2, blocks - 1))
        return carry

    lax.fori_loop(0, blocks // 2, pair, 0)
    hidden_rows = lax.dot_general(
        member_f32, hidden_sum_ref[...], last, precision=HIGHEST, preferred_element_type=F32
    )
    inverse = 1.0 / (height * TILE)
    branch = jnp.dot(
        hidden_rows * inverse, down_ref[...].astype(F32), precision=HIGHEST, preferred_element_type=F32
    ) + row_vectors_ref[1:2, :]
    features = lax.dot_general(
        member_f32, feature_sum_ref[...], last, precision=HIGHEST, preferred_element_type=F32
    )
    embedding_ref[...] = features * inverse + scaled_mask * branch
    down_sum = lax.dot_general(
        branch_rows.astype(F32), hidden_rows * scale, first, precision=HIGHEST, preferred_element_type=F32
    )
    across = hidden_units // LANES
    half = (channels // 8) * across
    for r in range(channels // 8):
        for k in range(across):
            at = (r * across + k) * 8
            cols = slice(k * LANES, (k + 1) * LANES)
            part_ref[at : at + 8, :] = up_sum_ref[8 * r : 8 * r + 8, cols] * scale
            part_ref[half * 8 + at : half * 8 + at + 8, :] = down_sum[8 * r : 8 * r + 8, cols]


def kernel_grad_kernel(
    top_ref, mid_ref, bottom_ref, grad_ref, out_ref, wide_ref, wide_grad_ref, tiles_ref, *, scale, lane0
):
    height, channels, _ = mid_ref.shape
    widen(top_ref, mid_ref, bottom_ref, wide_ref)

    def copy(r, carry):
        wide_grad_ref[r] = grad_ref[r].astype(F32)
        return carry

    lax.fori_loop(0, height, copy, 0)
    lanes = lane_ids(8)

    def conv(block, carry):
        c0 = pl.multiple_of(block * 8, 8)
        for b in range(7):
            shift = b - 3
            sums = [None] * 7
            for i in range(height):
                grad = wide_grad_ref[i, pl.ds(c0, 8), :]
                if shift != 0:
                    grad = pltpu.roll(grad, shift % LANES, 1)
                for a in range(7):
                    term = grad * wide_ref[i + a, pl.ds(c0, 8), :]
                    sums[a] = term if i == 0 else sums[a] + term
            for a in range(7):
                tiles_ref[7 * a + b] = sums[a]
        out = jnp.zeros((8, LANES), F32)
        for tap in range(49):
            shift = tap % 7 - 3
            total = tiles_ref[tap]
            if shift > 0:
                total = jnp.where(lanes >= shift, total, 0.0)
            elif shift < 0:
                total = jnp.where(lanes < LANES + shift, total, 0.0)
            total = jnp.sum(total, axis=1, keepdims=True)
            out = jnp.where(lanes == lane0 + tap, total, out)
        out_ref[pl.ds(c0, 8), :] = out * scale
        return carry

    lax.fori_loop(0, channels // 8, conv, 0)


def input_grad_kernel(
    top_ref, mid_ref, bottom_ref, taps_ref, cotangent_ref, out_ref, wide_ref, spread_ref, sum_ref
):
    height, channels, _ = mid_ref.shape
    widen(top_ref, mid_ref, bottom_ref, wide_ref)

    def conv(block, carry):
        c0 = pl.multiple_of(block * 8, 8)
        spread_taps(taps_ref[pl.ds(c0, 8), :], spread_ref, True)
        cotangent = cotangent_ref[pl.ds(c0, 8), :]

        def store(i, value):
            sum_ref[pl.ds(i, 8, stride=height), :] = value + cotangent

        depthwise(wide_ref, spread_ref, c0, store, height)
        at = pl.multiple_of(c0 * height, 8 * height)
        out_ref[pl.ds(at, 8 * height), :] = sum_ref[...].astype(BF16)
        return carry

    lax.fori_loop(0, channels // 8, conv, 0)


CONV_COST = 0.01
CONV_MIB = 58


def cost(us):
    return pl.CostEstimate(flops=int(us * 1.0e9), bytes_accessed=1 << 20, transcendentals=0)


def whole(x):
    return (x, x.shape, None, 0)


def part_of(x, dim, size, k):
    return (x, tuple(size if d == dim else n for d, n in enumerate(x.shape)), dim, k)


def call(kernel, operands, shapes, scratch, us, name, mib=40):
    def spec(shape, dim=None, k=0):
        return pl.BlockSpec(shape, lambda i: tuple(k if d == dim else 0 for d in range(len(shape))))

    return pl.pallas_call(
        kernel,
        grid=(1,),
        in_specs=[spec(*operand[1:]) for operand in operands],
        out_specs=[spec(shape) for shape, _ in shapes],
        out_shape=[jax.ShapeDtypeStruct(*shape) for shape in shapes],
        scratch_shapes=scratch,
        compiler_params=pltpu.CompilerParams(vmem_limit_bytes=mib << 20),
        cost_estimate=cost(us),
        name=name,
    )(*[operand[0] for operand in operands])


def after(xs, *others):
    return lax.optimization_barrier((tuple(xs), others))[0]


def patterns(bits):
    return [sum(bit for k, bit in enumerate(bits) if (p >> k) & 1) for p in range(1, 1 << len(bits))]


def exchange(x, axis, pattern):
    return lax.ppermute(x, axis, [(i, i ^ pattern) for i in range(lax.axis_size(axis))])


def rank_in(axis, bits):
    index = lax.axis_index(axis)
    return sum(((index // bit) % 2) * (1 << k) for k, bit in enumerate(bits))


def run(x, k, count):
    size = x.shape[0] // count
    return lax.dynamic_slice_in_dim(x, k * size, size)


def tree(parts):
    while len(parts) > 1:
        parts = [parts[k] + parts[k + 1] for k in range(0, len(parts), 2)]
    return parts[0]


def send_parts(x, axis, bits):
    me = rank_in(axis, bits)
    count = 1 << len(bits)
    sent = [exchange(run(x, me ^ (k + 1), count), axis, p) for k, p in enumerate(patterns(bits))]
    return [run(x, me, count)] + sent


def send_all(x, axis, bits):
    return [x] + [exchange(x, axis, p) for p in patterns(bits)]


def in_order(parts, axis, bits):
    me = rank_in(axis, bits)
    size = parts[0].shape[0]
    out = jnp.zeros((size * len(parts),) + parts[0].shape[1:], parts[0].dtype)
    for k, part in enumerate(parts):
        out = lax.dynamic_update_slice_in_dim(out, part, (me ^ k) * size, 0)
    return out


def halves(x):
    high = lax.reduce_precision(x, 8, 7)
    return high.astype(BF16), (x - high).astype(BF16)


def joined(x):
    size = x.shape[0] // 2
    return x[:size].astype(F32) + x[size:].astype(F32)


def edges(rows):
    count = lax.axis_size("rows")
    even = lax.axis_index("rows") % 2 == 0
    first, last = rows[:3], rows[-3:]
    a = exchange(jnp.where(even, last, first), "rows", 1)
    pairs = [(i, i + 1) for i in range(1, count - 1, 2)]
    b = lax.ppermute(jnp.where(even, first, last), "rows", pairs + [(j, i) for i, j in pairs])
    return jnp.where(even, b, a), jnp.where(even, a, b)


def on_device(
    features,
    depth_kernel,
    depth_bias,
    norm_gain,
    norm_bias,
    up_weight,
    up_bias,
    down_weight,
    down_bias,
    layer_scale,
    tissue,
    aggregator_order,
    tile_cotangent,
):
    channels, height, across = features.shape[1:]
    hidden_units = up_weight.shape[1]
    row_count = lax.axis_size("rows")
    tiles_here = across // TILE
    scale = 1.0 / math.sqrt(lax.axis_size("slide") * row_count * height * across)

    first_rows = features[0, :, :3].transpose(1, 0, 2)
    last_rows = features[0, :, -3:].transpose(1, 0, 2)
    top, bottom = edges(jnp.concatenate([first_rows, last_rows], axis=0))
    image = features[0].transpose(1, 0, 2)
    image_shape = (height, channels, across)
    vectors = jnp.stack([depth_bias, norm_gain, norm_bias], axis=1)
    spread = pltpu.VMEM((49, 8, LANES), F32)
    sent = jnp.broadcast_to(tile_cotangent, (row_count,) + tile_cotangent.shape[1:])
    cotangents = lax.all_to_all(sent, "rows", 0, 0, tiled=True).reshape(-1, channels)
    convolved, feature_sum = call(
        forward_kernel,
        [whole(x) for x in (top, image, bottom, depth_kernel, vectors)],
        [(image_shape, F32), ((channels, across), F32)],
        [pltpu.VMEM((height + 6, channels, across), F32), spread],
        CONV_COST,
        "convolution",
        CONV_MIB,
    )
    me = lax.axis_index("rows")
    positions = lax.dynamic_slice_in_dim(aggregator_order[0], me * tiles_here, tiles_here)
    meta = jnp.pad(jnp.stack([positions, tissue[0, 0]], axis=1), ((0, 8 - tiles_here), (0, 0)))
    row_vectors = jnp.stack([layer_scale, down_bias], axis=0)

    part_rows = 2 * channels * hidden_units // LANES
    operands = (
        convolved, feature_sum, cotangents, meta, vectors, row_vectors,
        up_weight, up_weight.T, down_weight, up_bias[:, None],
    )
    grad_conv, part, embedding, cotangent = call(
        functools.partial(mlp_kernel, scale=scale),
        [whole(x) for x in operands],
        [(image_shape, BF16), ((part_rows, LANES), F32), ((8, channels), F32), ((channels, across), F32)],
        [
            pltpu.VMEM((2, hidden_units, 2 * LANES), F32),
            pltpu.VMEM((2, hidden_units, 2 * LANES), BF16),
            pltpu.VMEM((hidden_units, LANES), F32),
            pltpu.VMEM((hidden_units, LANES), F32),
            pltpu.VMEM((hidden_units, LANES), F32),
            pltpu.VMEM((channels, hidden_units), F32),
            pltpu.VMEM((2, channels, LANES), F32),
            pltpu.VMEM((2, channels, 2 * LANES), BF16),
            pltpu.VMEM((2, 2, channels, LANES), F32),
            pltpu.VMEM((2, 2, LANES), F32),
        ],
        25,
        "mlp_both_ways",
    )

    grad_top, grad_bottom = edges(grad_conv)
    quarter = channels // 4
    wide = pltpu.VMEM((height + 6, quarter, across), F32)

    def kernel_piece(k, *gates):
        grad = after([grad_conv], *gates)[0]
        operands = [part_of(x, 1, quarter, k) for x in (top, image, bottom, grad)]
        return call(
            functools.partial(kernel_grad_kernel, scale=scale, lane0=LANES // 2 * (k // 2)),
            operands,
            [((quarter, LANES), F32)],
            [wide, pltpu.VMEM((height, quarter, across), F32), spread],
            4,
            "kernel_grad",
        )[0]

    def input_piece(k, *gates):
        grad = after([grad_conv], *gates)[0]
        operands = [part_of(x, 1, quarter, k) for x in (grad_top, grad, grad_bottom)]
        return call(
            input_grad_kernel,
            operands + [part_of(x, 0, quarter, k) for x in (depth_kernel, cotangent)],
            [((quarter * height, across), BF16)],
            [wide, spread, pltpu.VMEM((8 * height, across), F32)],
            4,
            "input_grad",
        )[0]

    terms = [kernel_piece(0)]
    part = after([part], grad_top, grad_bottom, terms[0])[0]
    terms.append(kernel_piece(1, grad_top, grad_bottom, terms[0]))
    own = tree(after(send_parts(part, "slide", (1,)), terms[1]))
    terms.append(kernel_piece(2, own))
    own = tree(after(send_parts(own, "rows", (1, 2)), terms[2]))
    terms.append(kernel_piece(3, own))
    own = tree(after(send_parts(own, "rows", (8, 16)), terms[3]))
    size = own.shape[0]
    taps = jnp.concatenate([terms[0] + terms[2], terms[1] + terms[3]], axis=0)
    own = jnp.concatenate([own, taps], axis=0)
    grads = []
    for axis, bit in (("rows", 32), ("rows", 4), ("slide", 2)):
        grads.append(input_piece(len(grads), own))
        own = tree(after(send_all(own, axis, (bit,)), grads[-1]))
    grads.append(input_piece(3, own))
    parts = after(send_all(own, "rows", (8, 16)), grads[3])
    taps = tree([x[size:] for x in parts])
    own = in_order([x[:size] for x in parts], "rows", (8, 16)).astype(BF16)
    size = 4 * size
    own = jnp.concatenate([own, *halves(taps)], axis=0)
    parts = send_all(own, "rows", (1, 2))
    taps = tree([joined(x[size:]) for x in parts])
    own = in_order([x[:size] for x in parts], "rows", (1, 2))
    size = 4 * size
    own = jnp.concatenate([own, *halves(taps)], axis=0)
    there = exchange(own, "slide", 1)
    low = rank_in("slide", (1,)) == 0
    first = jnp.where(low, own[:size], there[:size]).astype(F32)
    second = jnp.where(low, there[:size], own[:size]).astype(F32)
    taps = joined(own[size:]) + joined(there[size:])

    def untile(x):
        tiled = x.reshape(channels // 8, hidden_units // LANES, 8, LANES)
        return tiled.transpose(0, 2, 1, 3).reshape(channels, hidden_units)

    grad_kernel = jnp.concatenate([taps[:, :49], taps[:, LANES // 2 : LANES // 2 + 49]], axis=0)
    input_grad = jnp.concatenate(grads, axis=0).reshape((1, channels, height, across))
    return (embedding[None, :tiles_here], input_grad, untile(first), untile(second).T, grad_kernel)


def solution(mesh):
    return jax.shard_map(
        on_device,
        mesh=mesh,
        in_specs=(
            P("slide", None, "rows", None),
            P(),
            P(),
            P(),
            P(),
            P(),
            P(),
            P(),
            P(),
            P(),
            P("slide", "rows", None),
            P("slide", None),
            P("slide", "rows", None),
        ),
        out_specs=(P("slide", "rows", None), P("slide", None, "rows", None), P(), P(), P()),
        check_vma=False,
    )
```
